256 devices in a mesh: section: 4 (over z_lo), ty: 8 (over y, core), tx: 8 (over z_hi, x).
Axes of the slice: x: 4, y: 4, z: 8 (z_hi: 2, z_lo: 4; z = z_hi * 4 + z_lo), core: 2. Of those that a mesh axis runs over, the one named last changes fastest.
Arguments:
- acts: float32 [4, 1, 96, 64, 1024], P('section', None, None, 'ty', 'tx'), may hold values from -6 to 6
- top_grad: float32 [1, 96, 64, 1024], P(None, None, 'ty', 'tx'), may hold values from -6 to 6
- kernel: float32 [4, 49, 96], P('section'), may hold values from -0.875 to 0.875
- ln_gain: float32 [4, 96], P('section'), may hold values from 0.5 to 1.5
- ln_bias: float32 [4, 96], P('section'), may hold values from -3 to 3
- w_in: float32 [4, 96, 384], P('section'), may hold values from -0.625 to 0.625
- b_in: float32 [4, 384], P('section'), may hold values from -3 to 3
- w_out: float32 [4, 384, 96], P('section'), may hold values from -0.3125 to 0.3125
- layer_scale: float32 [4, 96], P('section'), may hold values from 0.3 to 1.5
Outputs:
- input_grad: float32 [4, 1, 96, 64, 1024], P('section', None, None, 'ty', 'tx')
- grad_kernel: float32 [4, 49, 96], P('section')
- grad_gain: float32 [4, 96], P('section')
- grad_bias: float32 [4, 96], P('section')
- grad_w_in: float32 [4, 96, 384], P('section')
- grad_b_in: float32 [4, 384], P('section')
- grad_w_out: float32 [4, 384, 96], P('section')
- grad_scale: float32 [4, 96], P('section')
The draws below stay inside these ranges and needn't reach their ends.
All inputs are finite; a program needn't handle non-finite values.
Results may differ from the reference program's by a relative error of at most 0.0001.
Values sent between devices are 32-bit elements; how exact they have to be, the bound alone decides.
No kernel may reach another device: no remote copies, remote signals or barrier semaphores. Data moves between devices by JAX's collectives and lax.ppermute only.
A program may use at most 128 MiB of HBM per device.

```python
import math
import jax
import jax.numpy as jnp
from jax import lax

C = 96
HID = 384
KS = 7
MB = 1
H = 64
W = 1024
N_SECTION = 4


def shard_levels(rng, dims, cuts, smallest, high):
    def one(dim, shards_of):
        steps = jax.random.uniform(jax.random.fold_in(jax.random.fold_in(rng, 6), dim), (shards_of,), jnp.float32, smallest / len(cuts), high / len(cuts))
        return jnp.repeat(jnp.exp(steps), dims[dim] // shards_of).reshape((-1,) + (1,) * (len(dims) - dim - 1))

    level = one(*cuts[0])
    for cut in cuts[1:]:
        level = level * one(*cut)
    return level


def bell_draw(own_key, shape, scale, most, shards=(), dtype=jnp.bfloat16):
    values = scale * jax.random.normal(own_key, shape, jnp.float32)
    if shards:
        values = values * shard_levels(own_key, shape, shards, -0.22, 0.18)
    return jnp.clip(values, -most, most).astype(dtype)


def setup_inputs(seed: int = 0) -> dict:
    streams_of = jax.random.split(jax.random.key(seed), 10)
    acts = bell_draw(streams_of[0], (N_SECTION, MB, C, H, W), 1.0, 6.0, ((0, 4), (3, 8), (4, 8)), jnp.float32)
    top_grad = bell_draw(streams_of[1], (MB, C, H, W), 1.0, 6.0, ((2, 8), (3, 8)), jnp.float32)
    kernel = bell_draw(streams_of[2], (N_SECTION, KS * KS, C), (KS * KS) ** -0.5, 0.875, ((0, 4),), jnp.float32)
    ln_gain = jnp.clip(1.0 + 0.1 * jax.random.normal(streams_of[3], (N_SECTION, C), jnp.float32), 0.5, 1.5)
    ln_bias = bell_draw(streams_of[4], (N_SECTION, C), 0.5, 3.0, ((0, 4),), jnp.float32)
    w_in = bell_draw(streams_of[5], (N_SECTION, C, HID), C ** -0.5, 0.625, ((0, 4),), jnp.float32)
    b_in = bell_draw(streams_of[6], (N_SECTION, HID), 0.5, 3.0, ((0, 4),), jnp.float32)
    w_out = bell_draw(streams_of[7], (N_SECTION, HID, C), HID ** -0.5, 0.3125, ((0, 4),), jnp.float32)
    layer_scale = jnp.clip(jnp.exp(math.log(1.5) - 1.60943787 * jax.random.uniform(streams_of[8], (N_SECTION, C), jnp.float32) ** shard_levels(streams_of[8], (N_SECTION, C), ((0, 4),), -0.2, 0.2)), 0.3, 1.5)
    return {"acts": acts, "top_grad": top_grad, "kernel": kernel, "ln_gain": ln_gain, "ln_bias": ln_bias, "w_in": w_in, "b_in": b_in, "w_out": w_out, "layer_scale": layer_scale}


HIGHEST = lax.Precision.HIGHEST
EPSILON = 1e-06

def depthwise(kernel, field):
    rows = field.shape[1]
    columns = field.shape[2]
    reach = KS // 2
    padded = jnp.pad(field, ((0, 0), (reach, reach), (reach, reach)))
    result = jnp.zeros(field.shape, jnp.float32)
    for offset_row in range(KS):
        for offset_col in range(KS):
            result = result + kernel[offset_row * KS + offset_col][:, None, None] * padded[:, offset_row:offset_row + rows, offset_col:offset_col + columns]
    return result

def block(params, field):
    kernel, gain, shift_bias, weight_in, bias_in, weight_out, scale = params
    conv_out = depthwise(kernel, field)
    centre = lax.optimization_barrier(jnp.mean(conv_out, axis=0))
    spread = lax.optimization_barrier(jnp.mean((conv_out - centre) ** 2, axis=0))
    normed = (conv_out - centre) * lax.rsqrt(spread + EPSILON)
    lifted = normed * gain[:, None, None] + shift_bias[:, None, None]
    pre_act = jnp.einsum('ch,cij->hij', weight_in, lifted, precision=HIGHEST) + bias_in[:, None, None]
    hidden = jax.nn.gelu(pre_act, approximate=False)
    branch = jnp.einsum('hc,hij->cij', weight_out, hidden, precision=HIGHEST)
    return field + scale[:, None, None] * branch

def reference(acts, top_grad, kernel, ln_gain, ln_bias, w_in, b_in, w_out, layer_scale):
    totals = [None] * N_SECTION
    grads_in = [[None] * MB for section_id in range(N_SECTION)]
    for micro in range(MB):
        cotan = top_grad[micro]
        for section_id in reversed(range(N_SECTION)):
            params = (kernel[section_id], ln_gain[section_id], ln_bias[section_id], w_in[section_id], b_in[section_id], w_out[section_id], layer_scale[section_id])
            unused, pullback = jax.vjp(block, params, acts[section_id, micro])
            param_grads, cotan = pullback(cotan)
            grads_in[section_id][micro] = cotan
            if totals[section_id] is None:
                totals[section_id] = param_grads
            else:
                totals[section_id] = jax.tree.map(lambda left, right: left + right, totals[section_id], param_grads)
    input_grad = jnp.stack([jnp.stack(grads_in[section_id]) for section_id in range(N_SECTION)])
    stacked = [jnp.stack([totals[section_id][index] for section_id in range(N_SECTION)]) for index in range(7)]
    return (input_grad, stacked[0], stacked[1], stacked[2], stacked[3], stacked[4], stacked[5], stacked[6])
```

```python
import jax
import jax.numpy as jnp
from jax import lax
from jax.sharding import PartitionSpec as P

KS = 7


HIGHEST = lax.Precision.HIGHEST
EPSILON = 1e-06
LANES = 128


def with_halo(value, sides, width):
    for axis, dim in sides:
        size, length = (lax.axis_size(axis), value.shape[dim])
        up = [(i, (i + 1) % size) for i in range(size - 1)]
        down = [(j, i) for i, j in up]
        last = lax.slice_in_dim(value, length - width, length, axis=dim)
        initial = lax.slice_in_dim(value, 0, width, axis=dim)
        before = lax.ppermute(last, axis, up)
        after = lax.ppermute(initial, axis, down)
        value = jnp.concatenate([before, value, after], axis=dim)
    return value


def from_behind(block, axis, distance):
    devices = range(lax.axis_size(axis))
    route = [(i - distance, i) for i in devices if i - distance in devices]
    return lax.ppermute(block, axis, route)


def grouped_conv(padded, filters):
    channels = padded.shape[0]
    result = lax.conv_general_dilated(
        padded[None],
        filters,
        (1, 1),
        "VALID",
        dimension_numbers=("NCHW", "OIHW", "NCHW"),
        feature_group_count=channels,
        precision=HIGHEST,
    )
    return result[0]


def kernel_filters(kernel):
    channels = kernel.shape[1]
    return jnp.transpose(kernel).reshape(channels, 1, KS, KS)


def conv_forward(kernel, padded):
    return grouped_conv(padded, kernel_filters(kernel))


def conv_transpose(kernel, grad_padded):
    flipped = kernel_filters(kernel)[:, :, ::-1, ::-1]
    return grouped_conv(grad_padded, flipped)


def kernel_grad(grad_conv, padded):
    channels = grad_conv.shape[0]
    taps = grouped_conv(padded, grad_conv[:, None, :, :])
    return jnp.transpose(taps.reshape(channels, KS * KS))


def pointwise_backward(conv_field, cotan_field, weights, first_row, first_col, out_rows, out_cols):
    kernel, gain, shift_bias, weight_in, bias_in, weight_out, scale = weights
    channels = conv_field.shape[0]
    field_rows = conv_field.shape[1]
    field_cols = conv_field.shape[2]
    cells = field_rows * field_cols
    lanes = (cells + 127) // 128 * 128

    def flatten(field):
        return jnp.pad(field.reshape(channels, cells), ((0, 0), (0, lanes - cells)))

    position = jnp.arange(lanes, dtype=jnp.int32)
    row_of = position // field_cols
    col_of = position % field_cols
    inside = (
        (position < cells)
        & (row_of >= first_row)
        & (row_of < first_row + out_rows)
        & (col_of >= first_col)
        & (col_of < first_col + out_cols)
    )
    weight_mask = inside.astype(jnp.float32)[None, :]
    conv_out = flatten(conv_field)
    cotan = flatten(cotan_field)
    centre = jnp.mean(conv_out, axis=0)
    spread = jnp.mean((conv_out - centre) ** 2, axis=0)
    inv_std = lax.rsqrt(spread + EPSILON)
    normed = (conv_out - centre) * inv_std
    lifted = normed * gain[:, None] + shift_bias[:, None]
    pre_act = jnp.einsum("ch,cn->hn", weight_in, lifted, precision=HIGHEST) + bias_in[:, None]
    hidden = jax.nn.gelu(pre_act, approximate=False)
    slope = (
        0.5 * (1.0 + jax.scipy.special.erf(pre_act * 0.7071067811865476))
        + pre_act * jnp.exp(-0.5 * pre_act * pre_act) * 0.3989422804014327
    )
    branch = jnp.einsum("hc,hn->cn", weight_out, hidden, precision=HIGHEST)
    grad_branch = scale[:, None] * cotan
    grad_hidden = jnp.einsum("hc,cn->hn", weight_out, grad_branch, precision=HIGHEST)
    grad_pre = grad_hidden * slope
    grad_lifted = jnp.einsum("ch,hn->cn", weight_in, grad_pre, precision=HIGHEST)
    grad_normed = grad_lifted * gain[:, None]
    grad_conv = inv_std * (
        grad_normed
        - jnp.mean(grad_normed, axis=0)
        - normed * jnp.mean(grad_normed * normed, axis=0)
    )
    grad_pre_kept = grad_pre * weight_mask
    grad_lifted_kept = grad_lifted * weight_mask
    grad_scale = jnp.sum(cotan * branch * weight_mask, axis=1)
    grad_w_out = jnp.einsum("hn,cn->hc", hidden, grad_branch * weight_mask, precision=HIGHEST)
    grad_b_in = jnp.sum(grad_pre_kept, axis=1)
    grad_w_in = jnp.einsum("cn,hn->ch", lifted, grad_pre_kept, precision=HIGHEST)
    grad_gain = jnp.sum(grad_lifted_kept * normed, axis=1)
    grad_bias = jnp.sum(grad_lifted_kept, axis=1)
    grad_field = grad_conv[:, :cells].reshape(channels, field_rows, field_cols)
    return (grad_field, (grad_gain, grad_bias, grad_w_in, grad_b_in, grad_w_out, grad_scale))


def block_backward(field, cotan, weights):
    kernel = weights[0]
    out_rows = field.shape[1]
    out_cols = field.shape[2]
    reach = KS // 2
    padded = with_halo(field, (("ty", 1), ("tx", 2)), reach)
    conv_out = conv_forward(kernel, padded)
    grad_conv, others = pointwise_backward(conv_out, cotan, weights, 0, 0, out_rows, out_cols)
    grad_padded = with_halo(grad_conv, (("ty", 1), ("tx", 2)), reach)
    field_grad = cotan + conv_transpose(kernel, grad_padded)
    taps_grad = kernel_grad(grad_conv, padded)
    return (field_grad, (taps_grad,) + others)


def sum_over_tiles(terms):
    axes = ("ty", "tx")
    devices = lax.axis_size(axes)
    flat = jnp.concatenate([term.reshape(-1) for term in terms])
    rows = -(-flat.shape[0] // (devices * LANES))
    flat = jnp.pad(flat, (0, devices * rows * LANES - flat.shape[0]))
    shares = lax.all_to_all(flat.reshape(devices, rows, LANES), axes, 0, 0)
    share = jnp.sum(shares, axis=0)
    whole = lax.all_to_all(jnp.broadcast_to(share[None], shares.shape), axes, 0, 0)
    whole = whole.reshape(-1)
    sums, start = [], 0
    for term in terms:
        sums.append(whole[start : start + term.size].reshape(term.shape))
        start += term.size
    return tuple(sums)


def on_device(acts, top_grad, kernel, ln_gain, ln_bias, w_in, b_in, w_out, layer_scale):
    sections = lax.axis_size("section")
    section_id = lax.axis_index("section")
    weights = (kernel[0], ln_gain[0], ln_bias[0], w_in[0], b_in[0], w_out[0], layer_scale[0])
    micro_count = acts.shape[1]
    field_shape = acts.shape[2:]
    received = jnp.zeros(field_shape, jnp.float32)
    grads_out = jnp.zeros(acts.shape[1:], jnp.float32)
    totals = (jnp.zeros(kernel.shape[1:], jnp.float32),) + tuple(
        (
            jnp.zeros(array.shape[1:], jnp.float32)
            for array in (ln_gain, ln_bias, w_in, b_in, w_out, layer_scale)
        )
    )
    tick_count = micro_count + sections - 1
    for tick_index in range(tick_count):
        micro = tick_index - (sections - 1 - section_id)
        active = jnp.logical_and(micro >= 0, micro < micro_count)
        picked = jnp.clip(micro, 0, micro_count - 1)
        field = lax.dynamic_index_in_dim(acts[0], picked, 0, keepdims=False)
        top_now = lax.dynamic_index_in_dim(top_grad, picked, 0, keepdims=False)
        cotan = jnp.where(section_id == sections - 1, top_now, received)
        field_grad, param_grads = block_backward(field, cotan, weights)
        factor = active.astype(jnp.float32)
        totals = tuple((total + factor * term for total, term in zip(totals, param_grads)))
        updated = lax.dynamic_update_index_in_dim(grads_out, field_grad, picked, 0)
        grads_out = jnp.where(active, updated, grads_out)
        if tick_index + 1 < tick_count:
            received = from_behind(field_grad, "section", -1)
    totals = sum_over_tiles(totals)
    return (grads_out[None],) + tuple((total[None] for total in totals))


def solution(mesh):
    placed = (
        P("section", None, None, "ty", "tx"),
        P(None, None, "ty", "tx"),
        P("section", None, None),
        P("section", None),
        P("section", None),
        P("section", None, None),
        P("section", None),
        P("section", None, None),
        P("section", None),
    )
    return jax.shard_map(
        on_device,
        mesh=mesh,
        in_specs=placed,
        out_specs=(
            P("section", None, None, "ty", "tx"),
            P("section", None, None),
            P("section", None),
            P("section", None),
            P("section", None, None),
            P("section", None),
            P("section", None, None),
            P("section", None),
        ),
        check_vma=False,
    )
```

```python
import jax
import jax.numpy as jnp
from jax import lax
from jax.experimental import pallas as pl
from jax.experimental.pallas import tpu as pltpu
from jax.sharding import PartitionSpec as P

KS = 7
TAPS = KS * KS
REACH = KS // 2
EPSILON = 1e-06
LANES = 128
GROUP = 8
ROWS = 8
C = 96
HID = 384
CELLS = ROWS * LANES
FOLD = 24
CHUNK = 256
PAYLOAD_ROWS = 1024
F32 = jnp.float32
BF16 = jnp.bfloat16
TILES = ("ty", "tx")


def call(kernel, outs, *operands, scratch=()):
    whole = pl.BlockSpec(memory_space=pltpu.VMEM)
    return pl.pallas_call(
        kernel,
        out_shape=[jax.ShapeDtypeStruct(shape, F32) for shape in outs],
        in_specs=[whole] * len(operands),
        out_specs=[whole] * len(outs),
        scratch_shapes=[pltpu.VMEM(shape, F32) for shape in scratch],
        compiler_params=pltpu.CompilerParams(vmem_limit_bytes=28 * 1024 * 1024),
    )(*operands)


def roll(value, shift):
    return pltpu.roll(value, shift % LANES, 1)


def lane_of(rows):
    return lax.broadcasted_iota(jnp.int32, (rows, LANES), 1)


def block(row):
    return pl.ds(row * LANES, LANES)


def split(value):
    high = value.astype(BF16)
    low = (value - high.astype(F32)).astype(BF16)
    return high, low


def product(left, right, dims):
    def part(one, two):
        return lax.dot_general(one, two, (dims, ((), ())), preferred_element_type=F32)

    return part(left[0], right[0]) + (part(left[0], right[1]) + part(left[1], right[0]))


ROW_COL = ((1,), (0,))
COL_COL = ((0,), (0,))
ROW_ROW = ((1,), (1,))


def pack_edges(field_ref, right_ref, left_ref):
    lane = lane_of(FOLD)
    for edge, out_ref in ((LANES - REACH, right_ref), (0, left_ref)):
        folded = jnp.zeros((FOLD, LANES), F32)
        for quarter in range(C // FOLD):
            part = pl.ds(quarter * FOLD, FOLD)
            for row in range(ROWS):
                at = 32 * quarter + REACH * row
                moved = roll(field_ref[part, block(row)], at - edge)
                folded = jnp.where((lane >= at) & (lane < at + REACH), moved, folded)
        out_ref[...] = folded


def unfold(folded_ref, wide_ref):
    for quarter in range(C // FOLD):
        wide_ref[pl.ds(quarter * FOLD, FOLD), :] = roll(folded_ref[...], -32 * quarter)


def shifted_row(row, left, right, lane, distance):
    if distance > 0:
        return roll(jnp.where(lane < distance, right, row), -distance)
    if distance < 0:
        return roll(jnp.where(lane >= LANES + distance, left, row), -distance)
    return row


def left_edge(wide, row):
    return roll(wide, LANES - REACH - REACH * row)


def right_edge(wide, row):
    return roll(wide, -REACH * row)


def tap_of(taps, tap):
    return jnp.broadcast_to(taps[:, tap : tap + 1], (GROUP, LANES))


def take_field(acts_ref, field_ref, right_ref, left_ref):
    for row in range(ROWS):
        field_ref[:, block(row)] = acts_ref[pl.ds(row, C, stride=ROWS), :]
    pack_edges(field_ref, right_ref, left_ref)


def padded_rows(group, field_ref, above_ref, below_ref, wides):
    lefts = [ref[pl.ds(group, GROUP), :] for ref in wides[0::2]]
    rights = [ref[pl.ds(group, GROUP), :] for ref in wides[1::2]]
    rows = []
    for index in range(REACH):
        value = above_ref[pl.ds(index * C + group, GROUP), :]
        rows.append((value, lefts[0], rights[0], ROWS - REACH + index))
    for index in range(ROWS):
        rows.append((field_ref[pl.ds(group, GROUP), block(index)], lefts[1], rights[1], index))
    for index in range(REACH):
        value = below_ref[pl.ds(index * C + group, GROUP), :]
        rows.append((value, lefts[2], rights[2], index))
    return [(value, left_edge(left, at), right_edge(right, at)) for value, left, right, at in rows]


EDGE_ROWS = REACH * C


def unfold_six(own_left, own_right, above_ref, below_ref, wides):
    folded = (
        above_ref.at[pl.ds(EDGE_ROWS, FOLD), :],
        above_ref.at[pl.ds(EDGE_ROWS + FOLD, FOLD), :],
        own_left,
        own_right,
        below_ref.at[pl.ds(EDGE_ROWS, FOLD), :],
        below_ref.at[pl.ds(EDGE_ROWS + FOLD, FOLD), :],
    )
    for source, wide in zip(folded, wides):
        unfold(source, wide)


def forward(
    field_ref, left_ref, right_ref, above_ref, below_ref, taps_ref,
    gain_ref, bias_ref, w_in_ref, b_in_ref,
    normed_ref, inv_ref, slope_ref, hidden_ref,
    *wides,
):
    unfold_six(left_ref, right_ref, above_ref, below_ref, wides)
    lane = lane_of(GROUP)

    def conv_group(index, carry):
        group = pl.multiple_of(index * GROUP, GROUP)
        taps = taps_ref[pl.ds(group, GROUP), :]
        rows = padded_rows(group, field_ref, above_ref, below_ref, wides)
        sums = [jnp.zeros((GROUP, LANES), F32)] * ROWS
        for b in range(KS):
            moved = [shifted_row(*row, lane, b - REACH) for row in rows]
            for a in range(KS):
                weight = tap_of(taps, a * KS + b)
                sums = [total + weight * moved[row + a] for row, total in enumerate(sums)]
        for row in range(ROWS):
            normed_ref[pl.ds(group, GROUP), block(row)] = sums[row]
        return carry

    lax.fori_loop(0, C // GROUP, conv_group, 0)
    w_in = split(w_in_ref[...])
    for start in range(0, CELLS, CHUNK):
        cells = pl.ds(start, CHUNK)
        conv_out = normed_ref[:, cells]
        centred = conv_out - jnp.mean(conv_out, axis=0, keepdims=True)
        inv = lax.rsqrt(jnp.mean(centred * centred, axis=0, keepdims=True) + EPSILON)
        normed = centred * inv
        normed_ref[:, cells] = normed
        inv_ref[:, cells] = inv
        lifted = normed * gain_ref[...] + bias_ref[...]
        pre_act = product(w_in, split(lifted), COL_COL) + b_in_ref[...]
        gate = 0.5 * (1.0 + lax.erf(pre_act * 0.7071067811865476))
        hidden_ref[:, cells] = pre_act * gate
        slope_ref[:, cells] = gate + pre_act * jnp.exp(-0.5 * pre_act * pre_act) * 0.3989422804014327


def pointwise(
    cotan_of, cotan_ref, grad_pre_ref, normed_ref, inv_ref, slope_ref,
    gain_ref, w_in_ref, w_out_ref, scale_ref, grad_ref,
):
    w_out = split(w_out_ref[...] * scale_ref[...])
    w_in = split(w_in_ref[...] * gain_ref[...])
    for start in range(0, CELLS, CHUNK):
        cells = pl.ds(start, CHUNK)
        cotan = jnp.concatenate(
            [cotan_of(row) for row in range(start // LANES, (start + CHUNK) // LANES)], axis=1
        )
        cotan_ref[:, cells] = cotan
        grad_pre = product(w_out, split(cotan), ROW_COL) * slope_ref[:, cells]
        if grad_pre_ref is not None:
            grad_pre_ref[:, cells] = grad_pre
        grad_normed = product(w_in, split(grad_pre), ROW_COL)
        normed = normed_ref[:, cells]
        mean = jnp.mean(grad_normed, axis=0, keepdims=True)
        along = jnp.mean(grad_normed * normed, axis=0, keepdims=True)
        grad_ref[:, cells] = inv_ref[:, cells] * (grad_normed - mean - normed * along)


def first_step(
    top_ref, active_ref, normed_ref, inv_ref, slope_ref, gain_ref, w_in_ref, w_out_ref, scale_ref,
    cotan_ref, grad_ref, to_right_ref, to_left_ref,
):
    def cotan_of(row):
        return top_ref[pl.ds(row, C, stride=ROWS), :] * active_ref[...]

    pointwise(
        cotan_of, cotan_ref, None, normed_ref, inv_ref, slope_ref,
        gain_ref, w_in_ref, w_out_ref, scale_ref, grad_ref,
    )
    pack_edges(grad_ref, to_right_ref, to_left_ref)


def row_sum(main_ref, above_ref, below_ref, row):
    value = main_ref[:, block(row)]
    if row < REACH:
        value = value + above_ref[:, block(row)]
    if row >= ROWS - REACH:
        value = value + below_ref[:, block(row - ROWS + REACH)]
    return value


def middle_step(
    main_ref, above_ref, below_ref, normed_ref, inv_ref, slope_ref,
    gain_ref, w_in_ref, w_out_ref, scale_ref,
    cotan_ref, grad_ref, to_right_ref, to_left_ref,
):
    def cotan_of(row):
        return row_sum(main_ref, above_ref, below_ref, row)

    pointwise(
        cotan_of, cotan_ref, None, normed_ref, inv_ref, slope_ref,
        gain_ref, w_in_ref, w_out_ref, scale_ref, grad_ref,
    )
    pack_edges(grad_ref, to_right_ref, to_left_ref)


def last_step(
    main_ref, above_ref, below_ref, cotan0_ref, cotan1_ref, cotan2_ref,
    normed_ref, inv_ref, slope_ref, gain_ref, w_in_ref, w_out_ref, scale_ref,
    cotan_ref, grad_ref, to_right_ref, to_left_ref, grad_pre_ref,
):
    def cotan_of(row):
        at = (slice(None), block(row))
        return row_sum(main_ref, above_ref, below_ref, row) + (cotan0_ref[at] + cotan1_ref[at] + cotan2_ref[at])

    pointwise(
        cotan_of, cotan_ref, grad_pre_ref, normed_ref, inv_ref, slope_ref,
        gain_ref, w_in_ref, w_out_ref, scale_ref, grad_ref,
    )
    pack_edges(grad_ref, to_right_ref, to_left_ref)


def spread(
    cotan_ref, grad_ref, left_ref, right_ref, taps_ref, main_ref, up_ref, down_ref, wide_left, wide_right
):
    unfold(left_ref, wide_left)
    unfold(right_ref, wide_right)
    lane = lane_of(GROUP)

    def conv_group(index, carry):
        group = pl.multiple_of(index * GROUP, GROUP)
        channels = pl.ds(group, GROUP)
        taps = taps_ref[channels, :]
        left, right = wide_left[channels, :], wide_right[channels, :]
        rows = [
            (grad_ref[channels, block(row)], left_edge(left, row), right_edge(right, row))
            for row in range(ROWS)
        ]
        sums = [None] * (ROWS + 2 * REACH)
        for row in range(ROWS):
            sums[row + REACH] = cotan_ref[channels, block(row)]
        for b in range(KS):
            moved = [shifted_row(*row, lane, REACH - b) for row in rows]
            for a in range(KS):
                weight = tap_of(taps, a * KS + b)
                for row in range(ROWS):
                    term = weight * moved[row]
                    old = sums[row + a]
                    sums[row + a] = term if old is None else old + term
        for row in range(REACH):
            up_ref[channels, block(row)] = sums[row]
            down_ref[channels, block(row)] = sums[ROWS + REACH + row]
        for row in range(ROWS):
            main_ref[channels, block(row)] = sums[REACH + row]
        return carry

    lax.fori_loop(0, C // GROUP, conv_group, 0)


def finish_field(main_ref, above_ref, below_ref, out_ref):
    for row in range(ROWS):
        out_ref[pl.ds(row, C, stride=ROWS), :] = row_sum(main_ref, above_ref, below_ref, row)


LIFT_ROWS = C + GROUP
OUT_AT = 0
IN_AT = OUT_AT + C * HID // LANES
TAPS_AT = IN_AT + LIFT_ROWS * HID // LANES
USED_ROWS = TAPS_AT + C


def parameter_terms(
    field_ref, left_ref, right_ref, above_ref, below_ref, grad_ref, cotan_ref, hidden_ref, normed_ref, grad_pre_ref,
    payload_ref,
    *wides,
):
    unfold_six(left_ref, right_ref, above_ref, below_ref, wides)
    lane = lane_of(GROUP)

    def taps_group(index, carry):
        group = pl.multiple_of(index * GROUP, GROUP)
        rows = padded_rows(group, field_ref, above_ref, below_ref, wides)
        grads = [grad_ref[pl.ds(group, GROUP), block(row)] for row in range(ROWS)]
        result = jnp.zeros((GROUP, LANES), F32)
        for b in range(KS):
            moved = [shifted_row(*row, lane, b - REACH) for row in rows]
            for a in range(KS):
                terms = [grads[row] * moved[row + a] for row in range(ROWS)]
                while len(terms) > 1:
                    terms = [one + two for one, two in zip(terms[0::2], terms[1::2])]
                total = jnp.sum(terms[0], axis=1, keepdims=True)
                result = jnp.where(lane == a * KS + b, total, result)
        payload_ref[pl.ds(TAPS_AT + group, GROUP), :] = result
        return carry

    lax.fori_loop(0, C // GROUP, taps_group, 0)
    grad_w_out = product(split(cotan_ref[...]), split(hidden_ref[...]), ROW_ROW)
    ones = jnp.where(lax.broadcasted_iota(jnp.int32, (GROUP, CELLS), 0) == 0, 1.0, 0.0)
    lifted = jnp.concatenate([normed_ref[...], ones], axis=0)
    grad_w_in = product(split(lifted), split(grad_pre_ref[...]), ROW_ROW)
    for part in range(HID // LANES):
        payload_ref[pl.ds(OUT_AT + part * C, C), :] = grad_w_out[:, part * LANES : (part + 1) * LANES]
        payload_ref[pl.ds(IN_AT + part * LIFT_ROWS, LIFT_ROWS), :] = grad_w_in[:, part * LANES : (part + 1) * LANES]
    payload_ref[pl.ds(USED_ROWS, PAYLOAD_ROWS - USED_ROWS), :] = jnp.zeros((PAYLOAD_ROWS - USED_ROWS, LANES), F32)


def sum_shares(shares_ref, out_ref):
    devices, rows = out_ref.shape[0], out_ref.shape[1]

    def add(device, total):
        return total + shares_ref[device]

    total = lax.fori_loop(1, devices, add, shares_ref[0], unroll=7)

    def put(device, carry):
        out_ref[device] = total
        return carry

    lax.fori_loop(0, devices, put, 0, unroll=8)


def parameter_grads(
    payload_ref, gain_ref, bias_ref, w_in_ref, w_out_ref, scale_ref,
    kernel_out, gain_out, bias_out, w_in_out, b_in_out, w_out_out, scale_out,
):
    kernel_out[...] = payload_ref[pl.ds(TAPS_AT, C), :].T[:TAPS, :]
    grad_gain = jnp.zeros((C, 1), F32)
    grad_bias = jnp.zeros((C, 1), F32)
    grad_scale = jnp.zeros((1, C), F32)
    for part in range(HID // LANES):
        hidden = pl.ds(part * LANES, LANES)
        grad_out = payload_ref[pl.ds(OUT_AT + part * C, C), :].T
        grad_scale = grad_scale + jnp.sum(grad_out * w_out_ref[hidden, :], axis=0, keepdims=True)
        w_out_out[hidden, :] = grad_out * scale_ref[...]
        at = IN_AT + part * LIFT_ROWS
        grad_in = payload_ref[pl.ds(at, C), :]
        grad_b = payload_ref[pl.ds(at + C, 1), :]
        b_in_out[:, hidden] = grad_b
        w_in_out[:, hidden] = grad_in * gain_ref[...] + bias_ref[...] * grad_b
        w_in = w_in_ref[:, hidden]
        grad_gain = grad_gain + jnp.sum(w_in * grad_in, axis=1, keepdims=True)
        grad_bias = grad_bias + jnp.sum(w_in * grad_b, axis=1, keepdims=True)
    gain_out[...] = grad_gain
    bias_out[...] = grad_bias
    scale_out[...] = grad_scale


def exchange(to_next, to_previous, axis):
    size = lax.axis_size(axis)
    up = [(i, i + 1) for i in range(size - 1)]
    down = [(i + 1, i) for i in range(size - 1)]
    return lax.ppermute(to_next, axis, up), lax.ppermute(to_previous, axis, down)


def to_previous_section(block_, step):
    sections, tiles = lax.axis_size("section"), lax.axis_size("ty")
    route = [
        (section * tiles + tile, (section - 1) * tiles + tile + step)
        for section in range(1, sections)
        for tile in range(tiles)
        if 0 <= tile + step < tiles
    ]
    return lax.ppermute(block_, ("section", "ty"), route)


def sum_over_tiles(payload):
    devices = lax.axis_size(TILES)
    rows = PAYLOAD_ROWS // devices
    shares = lax.all_to_all(payload.reshape(devices, rows, LANES), TILES, 0, 0)
    (copies,) = call(sum_shares, [(devices, rows, LANES)], shares)
    return lax.all_to_all(copies, TILES, 0, 0).reshape(PAYLOAD_ROWS, LANES)


def on_device(acts, top_grad, kernel, ln_gain, ln_bias, w_in, b_in, w_out, layer_scale):
    sections = lax.axis_size("section")
    is_last = (lax.axis_index("section") == sections - 1).astype(F32)
    active = jnp.full((1, LANES), is_last, F32)
    taps = kernel[0].T
    gain, shift_bias, scale = (ln_gain.reshape(C, 1), ln_bias.reshape(C, 1), layer_scale)
    weight_in, weight_out = (w_in[0], w_out[0])
    field_shape, edge, side, wide = ((C, CELLS), (C, REACH * LANES), (FOLD, LANES), (C, LANES))

    field, to_right, to_left = call(take_field, [field_shape, side, side], acts.reshape(C * ROWS, LANES))
    left, right = exchange(to_right, to_left, "tx")

    def edge_rows(first):
        rows = [field[:, row * LANES : (row + 1) * LANES] for row in range(first, first + REACH)]
        return jnp.concatenate(rows + [left, right], axis=0)

    above, below = exchange(edge_rows(ROWS - REACH), edge_rows(0), "ty")
    around = (field, left, right, above, below)
    normed, inv, slope, hidden = call(
        forward,
        [field_shape, (1, CELLS), (HID, CELLS), (HID, CELLS)],
        *around, taps, gain, shift_bias, weight_in, b_in.reshape(HID, 1),
        scratch=[wide] * 6,
    )
    saved = (normed, inv, slope, gain, weight_in, weight_out, scale)
    step_outs = [field_shape, field_shape, side, side]

    cotans = []
    cotan, grad, to_right, to_left = call(first_step, step_outs, top_grad.reshape(C * ROWS, LANES), active, *saved)
    for step in range(1, sections + 1):
        grad_left, grad_right = exchange(to_right, to_left, "tx")
        main, up, down = call(
            spread, [field_shape, edge, edge], cotan, grad, grad_left, grad_right, taps, scratch=[wide] * 2
        )
        if step == sections:
            break
        cotans.append(cotan)
        from_below = to_previous_section(up, -1)
        from_above = to_previous_section(down, 1)
        arrived = to_previous_section(main, 0)
        if step < sections - 1:
            cotan, grad, to_right, to_left = call(middle_step, step_outs, arrived, from_above, from_below, *saved)
        else:
            cotan, grad, to_right, to_left, grad_pre = call(
                last_step, step_outs + [(HID, CELLS)], arrived, from_above, from_below, *cotans, *saved
            )
            (payload,) = call(
                parameter_terms, [(PAYLOAD_ROWS, LANES)],
                *around, grad, cotan, hidden, normed, grad_pre, scratch=[wide] * 6,
            )
    grad_above, grad_below = exchange(down, up, "ty")
    (input_grad,) = call(finish_field, [(C * ROWS, LANES)], main, grad_above, grad_below)
    payload = sum_over_tiles(payload)
    grad_kernel, grad_gain, grad_bias, grad_w_in, grad_b_in, grad_w_out, grad_scale = call(
        parameter_grads,
        [(TAPS, C), (C, 1), (C, 1), (C, HID), (1, HID), (HID, C), (1, C)],
        payload, gain, shift_bias, weight_in, weight_out, scale,
    )
    return (
        input_grad.reshape(1, 1, C, ROWS, LANES),
        grad_kernel[None],
        grad_gain.reshape(1, C),
        grad_bias.reshape(1, C),
        grad_w_in[None],
        grad_b_in,
        grad_w_out[None],
        grad_scale,
    )


def solution(mesh):
    placed = (
        P("section", None, None, "ty", "tx"),
        P(None, None, "ty", "tx"),
        P("section", None, None),
        P("section", None),
        P("section", None),
        P("section", None, None),
        P("section", None),
        P("section", None, None),
        P("section", None),
    )
    return jax.shard_map(
        on_device,
        mesh=mesh,
        in_specs=placed,
        out_specs=(
            P("section", None, None, "ty", "tx"),
            P("section", None, None),
            P("section", None),
            P("section", None),
            P("section", None, None),
            P("section", None),
            P("section", None, None),
            P("section", None),
        ),
        check_vma=False,
    )
```

```python
import functools

import jax
import jax.numpy as jnp
from jax import lax
from jax.experimental import pallas as pl
from jax.experimental.pallas import tpu as pltpu
from jax.sharding import PartitionSpec as P

KS = 7
TAPS = KS * KS
REACH = KS // 2
EPSILON = 1e-06
LANES = 128
GROUP = 8
ROWS = 8
C = 96
HID = 384
CELLS = ROWS * LANES
FOLD = 24
CHUNK = 256
PAYLOAD_ROWS = 1024
F32 = jnp.float32
BF16 = jnp.bfloat16
CONV_FLOPS = 2 * TAPS * C * CELLS
TILES = ("ty", "tx")


def call(kernel, outs, *operands, scratch=(), flops=0):
    whole = pl.BlockSpec(memory_space=pltpu.VMEM)
    return pl.pallas_call(
        kernel,
        out_shape=[jax.ShapeDtypeStruct(shape, F32) for shape in outs],
        in_specs=[whole] * len(operands),
        out_specs=[whole] * len(outs),
        scratch_shapes=[pltpu.VMEM(shape, F32) for shape in scratch],
        compiler_params=pltpu.CompilerParams(vmem_limit_bytes=28 * 1024 * 1024),
        cost_estimate=pl.CostEstimate(flops=flops, bytes_accessed=0, transcendentals=0) if flops else None,
    )(*operands)


def roll(value, shift):
    return pltpu.roll(value, shift % LANES, 1)


def lane_of(rows):
    return lax.broadcasted_iota(jnp.int32, (rows, LANES), 1)


def block(row):
    return pl.ds(row * LANES, LANES)


def split(value):
    high = value.astype(BF16)
    low = (value - high.astype(F32)).astype(BF16)
    return high, low


def product(left, right, dims):
    def part(one, two):
        return lax.dot_general(one, two, (dims, ((), ())), preferred_element_type=F32)

    return part(left[0], right[0]) + (part(left[0], right[1]) + part(left[1], right[0]))


ROW_COL = ((1,), (0,))
COL_COL = ((0,), (0,))
ROW_ROW = ((1,), (1,))


def pack_edges(field_ref, right_ref, left_ref):
    lane = lane_of(FOLD)
    for edge, out_ref in ((LANES - REACH, right_ref), (0, left_ref)):
        folded = jnp.zeros((FOLD, LANES), F32)
        for quarter in range(C // FOLD):
            part = pl.ds(quarter * FOLD, FOLD)
            for row in range(ROWS):
                at = 32 * quarter + REACH * row
                moved = roll(field_ref[part, block(row)], at - edge)
                folded = jnp.where((lane >= at) & (lane < at + REACH), moved, folded)
        out_ref[...] = folded


def unfold(folded_ref, wide_ref):
    for quarter in range(C // FOLD):
        wide_ref[pl.ds(quarter * FOLD, FOLD), :] = roll(folded_ref[...], -32 * quarter)


def shifted_row(row, left, right, lane, distance):
    if distance > 0:
        return roll(jnp.where(lane < distance, right, row), -distance)
    if distance < 0:
        return roll(jnp.where(lane >= LANES + distance, left, row), -distance)
    return row


def left_edge(wide, row):
    return roll(wide, LANES - REACH - REACH * row)


def right_edge(wide, row):
    return roll(wide, -REACH * row)


def tap_of(taps, tap):
    return jnp.broadcast_to(taps[:, tap : tap + 1], (GROUP, LANES))


def take_field(acts_ref, field_ref, right_ref, left_ref):
    for row in range(ROWS):
        field_ref[:, block(row)] = acts_ref[pl.ds(row, C, stride=ROWS), :]
    pack_edges(field_ref, right_ref, left_ref)


def column(row):
    return jnp.broadcast_to(row, (GROUP, row.shape[1])).T[:, :1]


def prepare(
    top_ref, active_ref, kernel_ref, gain_row, bias_row, w_in_ref, b_in_row, w_out_ref, scale_row,
    cotan_ref, taps_ref, gain_ref, bias_ref, b_in_ref, w_in_gain_ref, w_out_scale_ref,
):
    for row in range(ROWS):
        cotan_ref[:, block(row)] = top_ref[pl.ds(row, C, stride=ROWS), :] * active_ref[...]
    taps_ref[:, :TAPS] = kernel_ref[:, 0, :].T
    gain_ref[...] = column(gain_row[...])
    bias_ref[...] = column(bias_row[...])
    b_in_ref[...] = column(b_in_row[...])
    w_in_gain_ref[...] = w_in_ref[...] * gain_ref[...]
    w_out_scale_ref[...] = (w_out_ref[...] * column(scale_row[...])).T


def padded_rows(group, field_ref, above_ref, below_ref, wides):
    lefts = [ref[pl.ds(group, GROUP), :] for ref in wides[0::2]]
    rights = [ref[pl.ds(group, GROUP), :] for ref in wides[1::2]]
    rows = []
    for index in range(REACH):
        value = above_ref[pl.ds(index * C + group, GROUP), :]
        rows.append((value, lefts[0], rights[0], ROWS - REACH + index))
    for index in range(ROWS):
        rows.append((field_ref[pl.ds(group, GROUP), block(index)], lefts[1], rights[1], index))
    for index in range(REACH):
        value = below_ref[pl.ds(index * C + group, GROUP), :]
        rows.append((value, lefts[2], rights[2], index))
    return [(value, left_edge(left, at), right_edge(right, at)) for value, left, right, at in rows]


EDGE_ROWS = REACH * C


def unfold_six(own_left, own_right, above_ref, below_ref, wides):
    folded = (
        above_ref.at[pl.ds(EDGE_ROWS, FOLD), :],
        above_ref.at[pl.ds(EDGE_ROWS + FOLD, FOLD), :],
        own_left,
        own_right,
        below_ref.at[pl.ds(EDGE_ROWS, FOLD), :],
        below_ref.at[pl.ds(EDGE_ROWS + FOLD, FOLD), :],
    )
    for source, wide in zip(folded, wides):
        unfold(source, wide)


def tap_index(a, b, flipped):
    tap = a * KS + b
    return TAPS - 1 - tap if flipped else tap


def conv_own(flipped, *refs):
    start_ref = refs[0] if flipped else None
    field_ref, left_ref, right_ref, taps_ref, out_ref, wide_left, wide_right = refs[-7:]
    unfold(left_ref, wide_left)
    unfold(right_ref, wide_right)
    lane = lane_of(GROUP)

    def conv_group(index, carry):
        channels = pl.ds(pl.multiple_of(index * GROUP, GROUP), GROUP)
        taps = taps_ref[channels, :]
        left, right = wide_left[channels, :], wide_right[channels, :]
        rows = [
            (field_ref[channels, block(row)], left_edge(left, row), right_edge(right, row))
            for row in range(ROWS)
        ]
        if flipped:
            sums = [start_ref[channels, block(row)] for row in range(ROWS)]
        else:
            sums = [jnp.zeros((GROUP, LANES), F32)] * ROWS
        for b in range(KS):
            moved = [shifted_row(*row, lane, b - REACH) for row in rows]
            for a in range(KS):
                weight = tap_of(taps, tap_index(a, b, flipped))
                for row in range(ROWS):
                    if 0 <= row + a - REACH < ROWS:
                        sums[row] = sums[row] + weight * moved[row + a - REACH]
        for row in range(ROWS):
            out_ref[channels, block(row)] = sums[row]
        return carry

    lax.fori_loop(0, C // GROUP, conv_group, 0)


def conv_edges(flipped, own_ref, above_ref, below_ref, taps_ref, wides, put):
    sources = (
        above_ref.at[pl.ds(EDGE_ROWS, FOLD), :],
        above_ref.at[pl.ds(EDGE_ROWS + FOLD, FOLD), :],
        below_ref.at[pl.ds(EDGE_ROWS, FOLD), :],
        below_ref.at[pl.ds(EDGE_ROWS + FOLD, FOLD), :],
    )
    for source, wide in zip(sources, wides):
        unfold(source, wide)
    lane = lane_of(GROUP)

    def conv_group(index, carry):
        group = pl.multiple_of(index * GROUP, GROUP)
        channels = pl.ds(group, GROUP)
        taps = taps_ref[channels, :]
        edges = [wide[channels, :] for wide in wides]
        rows = []
        for side, ref in enumerate((above_ref, below_ref)):
            for at in range(REACH):
                theirs = at if side else ROWS - REACH + at
                mine = ROWS + at if side else at - REACH
                left, right = edges[2 * side], edges[2 * side + 1]
                value = ref[pl.ds(at * C + group, GROUP), :]
                rows.append((mine, (value, left_edge(left, theirs), right_edge(right, theirs))))
        sums = [own_ref[channels, block(row)] for row in range(ROWS)]
        for b in range(KS):
            moved = {mine: shifted_row(*row, lane, b - REACH) for mine, row in rows}
            for a in range(KS):
                if a == REACH:
                    continue
                weight = tap_of(taps, tap_index(a, b, flipped))
                for row in range(ROWS):
                    if row + a - REACH in moved:
                        sums[row] = sums[row] + weight * moved[row + a - REACH]
        put(group, sums)
        return carry

    lax.fori_loop(0, C // GROUP, conv_group, 0)


def forward(
    own_ref, above_ref, below_ref, taps_ref, gain_ref, bias_ref, w_in_ref, b_in_ref,
    normed_ref, inv_ref, slope_ref, hidden_ref,
    *wides,
):
    def put(group, sums):
        for row in range(ROWS):
            normed_ref[pl.ds(group, GROUP), block(row)] = sums[row]

    conv_edges(False, own_ref, above_ref, below_ref, taps_ref, wides, put)
    w_in = split(w_in_ref[...])
    for start in range(0, CELLS, CHUNK):
        cells = pl.ds(start, CHUNK)
        conv_out = normed_ref[:, cells]
        centred = conv_out - jnp.mean(conv_out, axis=0, keepdims=True)
        inv = lax.rsqrt(jnp.mean(centred * centred, axis=0, keepdims=True) + EPSILON)
        normed = centred * inv
        normed_ref[:, cells] = normed
        inv_ref[:, cells] = inv
        lifted = normed * gain_ref[...] + bias_ref[...]
        pre_act = product(w_in, split(lifted), COL_COL) + b_in_ref[...]
        gate = 0.5 * (1.0 + lax.erf(pre_act * 0.7071067811865476))
        hidden_ref[:, cells] = pre_act * gate
        slope_ref[:, cells] = gate + pre_act * jnp.exp(-0.5 * pre_act * pre_act) * 0.3989422804014327


def step(
    cotan_refs, normed_ref, inv_ref, slope_ref, w_in_gain_ref, w_out_scale_ref,
    grad_ref, to_right_ref, to_left_ref, cotan_ref=None, grad_pre_ref=None,
):
    w_out = split(w_out_scale_ref[...])
    w_in = split(w_in_gain_ref[...])
    for start in range(0, CELLS, CHUNK):
        cells = pl.ds(start, CHUNK)
        cotan = sum(ref[:, cells] for ref in cotan_refs)
        grad_pre = product(w_out, split(cotan), ROW_COL) * slope_ref[:, cells]
        if grad_pre_ref is not None:
            cotan_ref[:, cells] = cotan
            grad_pre_ref[:, cells] = grad_pre
        grad_normed = product(w_in, split(grad_pre), ROW_COL)
        normed = normed_ref[:, cells]
        mean = jnp.mean(grad_normed, axis=0, keepdims=True)
        along = jnp.mean(grad_normed * normed, axis=0, keepdims=True)
        grad_ref[:, cells] = inv_ref[:, cells] * (grad_normed - mean - normed * along)
    pack_edges(grad_ref, to_right_ref, to_left_ref)


def middle_step(cotan_ref, *refs):
    step((cotan_ref,), *refs)


def last_step(count, *refs):
    step(refs[:count], *refs[count:])


def finish(own_ref, above_ref, below_ref, taps_ref, out_ref, *wides):
    def put(group, sums):
        for row in range(ROWS):
            out_ref[pl.ds(group, GROUP), block(row)] = sums[row]

    conv_edges(True, own_ref, above_ref, below_ref, taps_ref, wides, put)


def last_finish(own_ref, above_ref, below_ref, taps_ref, out_ref, *wides):
    def put(group, sums):
        for row in range(ROWS):
            out_ref[pl.ds(group * ROWS + row, GROUP, stride=ROWS), :] = sums[row]

    conv_edges(True, own_ref, above_ref, below_ref, taps_ref, wides, put)


LIFT_ROWS = C + GROUP
OUT_AT = 0
IN_AT = OUT_AT + C * HID // LANES
TAPS_AT = IN_AT + LIFT_ROWS * HID // LANES
USED_ROWS = TAPS_AT + C


def parameter_terms(
    field_ref, left_ref, right_ref, above_ref, below_ref, grad_ref, cotan_ref, hidden_ref, normed_ref, grad_pre_ref,
    payload_ref,
    *wides,
):
    unfold_six(left_ref, right_ref, above_ref, below_ref, wides)
    lane = lane_of(GROUP)

    def taps_group(index, carry):
        group = pl.multiple_of(index * GROUP, GROUP)
        rows = padded_rows(group, field_ref, above_ref, below_ref, wides)
        grads = [grad_ref[pl.ds(group, GROUP), block(row)] for row in range(ROWS)]
        result = jnp.zeros((GROUP, LANES), F32)
        for b in range(KS):
            moved = [shifted_row(*row, lane, b - REACH) for row in rows]
            for a in range(KS):
                terms = [grads[row] * moved[row + a] for row in range(ROWS)]
                while len(terms) > 1:
                    terms = [one + two for one, two in zip(terms[0::2], terms[1::2])]
                total = jnp.sum(terms[0], axis=1, keepdims=True)
                result = jnp.where(lane == a * KS + b, total, result)
        payload_ref[pl.ds(TAPS_AT + group, GROUP), :] = result
        return carry

    lax.fori_loop(0, C // GROUP, taps_group, 0)
    grad_w_out = product(split(cotan_ref[...]), split(hidden_ref[...]), ROW_ROW)
    ones = jnp.where(lax.broadcasted_iota(jnp.int32, (GROUP, CELLS), 0) == 0, 1.0, 0.0)
    lifted = jnp.concatenate([normed_ref[...], ones], axis=0)
    grad_w_in = product(split(lifted), split(grad_pre_ref[...]), ROW_ROW)
    for part in range(HID // LANES):
        payload_ref[pl.ds(OUT_AT + part * C, C), :] = grad_w_out[:, part * LANES : (part + 1) * LANES]
        payload_ref[pl.ds(IN_AT + part * LIFT_ROWS, LIFT_ROWS), :] = grad_w_in[:, part * LANES : (part + 1) * LANES]
    payload_ref[pl.ds(USED_ROWS, PAYLOAD_ROWS - USED_ROWS), :] = jnp.zeros((PAYLOAD_ROWS - USED_ROWS, LANES), F32)


def sum_shares(shares_ref, out_ref):
    devices, rows = out_ref.shape[0], out_ref.shape[1]

    def add(device, total):
        return total + shares_ref[device]

    total = lax.fori_loop(1, devices, add, shares_ref[0], unroll=7)

    def put(device, carry):
        out_ref[device] = total
        return carry

    lax.fori_loop(0, devices, put, 0, unroll=8)


def parameter_grads(
    payload_ref, gain_ref, bias_ref, w_in_ref, w_out_ref, scale_row,
    kernel_out, gain_out, bias_out, w_in_out, b_in_out, w_out_out, scale_out,
):
    kernel_out[:, 0, :] = payload_ref[pl.ds(TAPS_AT, C), :].T[:TAPS, :]
    scale = column(scale_row[...])
    sums = [jnp.zeros((C, 1), F32)] * 3
    for part in range(HID // LANES):
        hidden = pl.ds(part * LANES, LANES)
        grad_out = payload_ref[pl.ds(OUT_AT + part * C, C), :]
        w_out_out[:, hidden] = grad_out * scale
        at = IN_AT + part * LIFT_ROWS
        grad_in = payload_ref[pl.ds(at, C), :]
        grad_b = payload_ref[pl.ds(at + C, 1), :]
        b_in_out[:, hidden] = grad_b
        w_in_out[:, hidden] = grad_in * gain_ref[...] + bias_ref[...] * grad_b
        w_in = w_in_ref[:, hidden]
        terms = (w_in * grad_in, w_in * grad_b, w_out_ref[:, hidden] * grad_out)
        sums = [total + jnp.sum(term, axis=1, keepdims=True) for total, term in zip(sums, terms)]
    for total, out in zip(sums, (gain_out, bias_out, scale_out)):
        out[...] = jnp.broadcast_to(total, (C, LANES)).T[:1, :]


def exchange(to_next, to_previous, axis, section=None):
    size = lax.axis_size(axis)
    sections = range(lax.axis_size("section")) if section is None else (section,)
    up = [(s * size + i, s * size + i + 1) for s in sections for i in range(size - 1)]
    down = [(there, here) for here, there in up]
    axes = ("section", axis)
    return lax.ppermute(to_next, axes, up), lax.ppermute(to_previous, axes, down)


def sum_over_tiles(payload):
    devices = lax.axis_size(TILES)
    rows = PAYLOAD_ROWS // devices
    shares = lax.all_to_all(payload.reshape(devices, rows, LANES), TILES, 0, 0)
    (copies,) = call(sum_shares, [(devices, rows, LANES)], shares)
    return lax.all_to_all(copies, TILES, 0, 0).reshape(PAYLOAD_ROWS, LANES)


def edge_rows(field, left, right, first):
    rows = [field[:, row * LANES : (row + 1) * LANES] for row in range(first, first + REACH)]
    return jnp.concatenate(rows + [left, right], axis=0)


def exchange_rows(field, left, right, section=None):
    return exchange(edge_rows(field, left, right, ROWS - REACH), edge_rows(field, left, right, 0), "ty", section)


def on_device(acts, top_grad, kernel, ln_gain, ln_bias, w_in, b_in, w_out, layer_scale):
    sections = lax.axis_size("section")
    is_last = (lax.axis_index("section") == sections - 1).astype(F32)
    active = jnp.full((1, LANES), is_last, F32)
    field_shape, side, wide, hidden_shape = ((C, CELLS), (FOLD, LANES), (C, LANES), (HID, CELLS))
    weight_in, weight_out = (w_in[0], w_out[0].T)
    acts_rows, top_rows = (acts.reshape(C * ROWS, LANES), top_grad.reshape(C * ROWS, LANES))

    field, to_right, to_left = call(take_field, [field_shape, side, side], acts_rows)
    left, right = exchange(to_right, to_left, "tx")
    cotan, taps, gain, shift_bias, bias_in, w_in_gain, w_out_scale = call(
        prepare,
        [field_shape, wide, (C, 1), (C, 1), (HID, 1), (C, HID), (HID, C)],
        top_rows, active, jnp.transpose(kernel, (1, 0, 2)), ln_gain, ln_bias, weight_in, b_in, weight_out, layer_scale,
    )
    above, below = exchange_rows(field, left, right)
    (own,) = call(
        functools.partial(conv_own, False), [field_shape], field, left, right, taps, scratch=[wide] * 2, flops=CONV_FLOPS
    )
    normed, inv, slope, hidden = call(
        forward,
        [field_shape, (1, CELLS), hidden_shape, hidden_shape],
        own, above, below, taps, gain, shift_bias, weight_in, bias_in,
        scratch=[wide] * 4,
    )
    saved = (normed, inv, slope, w_in_gain, w_out_scale)
    step_outs = [field_shape, side, side]

    cotans = [cotan]
    for section in reversed(range(sections)):
        if section:
            only = section
            grad, to_right, to_left = call(middle_step, step_outs, cotan, *saved)
        else:
            only = None
            grad, to_right, to_left, cotan, grad_pre = call(
                functools.partial(last_step, len(cotans)), step_outs + [field_shape, hidden_shape], *cotans, *saved
            )
        grad_left, grad_right = exchange(to_right, to_left, "tx", only)
        if not section:
            (payload,) = call(
                parameter_terms, [(PAYLOAD_ROWS, LANES)],
                field, left, right, above, below, grad, cotan, hidden, normed, grad_pre, scratch=[wide] * 6,
                flops=4 * CONV_FLOPS,
            )
        grad_above, grad_below = exchange_rows(grad, grad_left, grad_right, only)
        (own,) = call(
            functools.partial(conv_own, True), [field_shape],
            cotan, grad, grad_left, grad_right, taps, scratch=[wide] * 2, flops=CONV_FLOPS,
        )
        edges = (own, grad_above, grad_below, taps)
        if section:
            (cotan,) = call(finish, [field_shape], *edges, scratch=[wide] * 4)
            cotan = lax.ppermute(cotan, "section", [(section, section - 1)])
            cotans.append(cotan)
    (input_grad,) = call(last_finish, [(C * ROWS, LANES)], *edges, scratch=[wide] * 4)
    payload = sum_over_tiles(payload)
    grad_kernel, grad_gain, grad_bias, grad_w_in, grad_b_in, grad_w_out, grad_scale = call(
        parameter_grads,
        [(TAPS, 1, C), (1, C), (1, C), (C, HID), (1, HID), (C, HID), (1, C)],
        payload, gain, shift_bias, weight_in, weight_out, layer_scale,
    )
    return (
        input_grad.reshape(1, 1, C, ROWS, LANES),
        jnp.transpose(grad_kernel, (1, 0, 2)),
        grad_gain,
        grad_bias,
        grad_w_in[None],
        grad_b_in,
        grad_w_out.T[None],
        grad_scale,
    )


def solution(mesh):
    placed = (
        P("section", None, None, "ty", "tx"),
        P(None, None, "ty", "tx"),
        P("section", None, None),
        P("section", None),
        P("section", None),
        P("section", None, None),
        P("section", None),
        P("section", None, None),
        P("section", None),
    )
    return jax.shard_map(
        on_device,
        mesh=mesh,
        in_specs=placed,
        out_specs=(
            P("section", None, None, "ty", "tx"),
            P("section", None, None),
            P("section", None),
            P("section", None),
            P("section", None, None),
            P("section", None),
            P("section", None, None),
            P("section", None),
        ),
        check_vma=False,
    )
```

```python
import functools

import jax
import jax.numpy as jnp
from jax import lax
from jax.experimental import pallas as pl
from jax.experimental.pallas import tpu as pltpu
from jax.sharding import PartitionSpec as P

KS = 7
TAPS = KS * KS
REACH = KS // 2
EPSILON = 1e-06
LANES = 128
GROUP = 8
ROWS = 8
C = 96
HID = 384
CELLS = ROWS * LANES
FOLD = 24
CHUNK = 256
PAYLOAD_ROWS = 1024
F32 = jnp.float32
BF16 = jnp.bfloat16
CONV_FLOPS = 2 * TAPS * C * CELLS
TILES = ("ty", "tx")


def call(kernel, outs, *operands, scratch=(), flops=0, copied=False):
    whole = pl.BlockSpec(memory_space=pltpu.VMEM)
    specs = [
        pl.BlockSpec(memory_space=pltpu.SMEM if operand.dtype == jnp.int32 else pltpu.HBM if copied else pltpu.VMEM)
        for operand in operands
    ]
    spaces = [pltpu.VMEM(shape, F32) if isinstance(shape, tuple) else shape for shape in scratch]
    return pl.pallas_call(
        kernel,
        out_shape=[jax.ShapeDtypeStruct(shape, F32) for shape in outs],
        in_specs=specs,
        out_specs=[whole] * len(outs),
        scratch_shapes=spaces,
        compiler_params=pltpu.CompilerParams(vmem_limit_bytes=28 * 1024 * 1024),
        cost_estimate=pl.CostEstimate(flops=flops, bytes_accessed=0, transcendentals=0) if flops else None,
    )(*operands)


def roll(value, shift):
    return pltpu.roll(value, shift % LANES, 1)


def lane_of(rows):
    return lax.broadcasted_iota(jnp.int32, (rows, LANES), 1)


def block(row):
    return pl.ds(row * LANES, LANES)


def split(value):
    high = value.astype(BF16)
    low = (value - high.astype(F32)).astype(BF16)
    return high, low


def product(left, right, dims):
    def part(one, two):
        return lax.dot_general(one, two, (dims, ((), ())), preferred_element_type=F32)

    return part(left[0], right[0]) + (part(left[0], right[1]) + part(left[1], right[0]))


ROW_COL = ((1,), (0,))
COL_COL = ((0,), (0,))
ROW_ROW = ((1,), (1,))


def pack_edges(field_ref, right_ref, left_ref):
    lane = lane_of(FOLD)
    for edge, out_ref in ((LANES - REACH, right_ref), (0, left_ref)):
        folded = jnp.zeros((FOLD, LANES), F32)
        for quarter in range(C // FOLD):
            part = pl.ds(quarter * FOLD, FOLD)
            for row in range(ROWS):
                at = 32 * quarter + REACH * row
                moved = roll(field_ref[part, block(row)], at - edge)
                folded = jnp.where((lane >= at) & (lane < at + REACH), moved, folded)
        out_ref[...] = folded


SIDE = 32


def unfold(left, right, quarters, rows):
    lane = lane_of(rows)
    parts = []
    for quarter in range(quarters):
        theirs = roll(left, -32 * quarter)
        parts.append(jnp.where(lane < SIDE, theirs, jnp.where(lane < 2 * SIDE, roll(right, SIDE - 32 * quarter), 0.0)))
    return jnp.concatenate(parts, axis=0)


def shifted_row(row, left, right, lane, distance):
    if distance > 0:
        return roll(jnp.where(lane < distance, right, row), -distance)
    if distance < 0:
        return roll(jnp.where(lane >= LANES + distance, left, row), -distance)
    return row


def with_edges(value, strip, row):
    return value, roll(strip, LANES - REACH - REACH * row), roll(strip, -SIDE - REACH * row)


def tap_of(taps, tap):
    return jnp.broadcast_to(taps[:, tap : tap + 1], (GROUP, LANES))


def take_field(acts_ref, field_ref, right_ref, left_ref):
    for row in range(ROWS):
        field_ref[:, block(row)] = acts_ref[pl.ds(row, C, stride=ROWS), :]
    pack_edges(field_ref, right_ref, left_ref)


def column(row):
    return jnp.broadcast_to(row, (GROUP, row.shape[1])).T[:, :1]


def prepare(*refs):
    count = 8
    sources, outs, held = refs[: count], refs[count : -count - 1], refs[-count - 1 : -1]
    sems = refs[-1]
    copies = [pltpu.make_async_copy(source, target, sems.at[i]) for i, (source, target) in enumerate(zip(sources, held))]
    for copy in copies:
        copy.start()
    for copy in copies:
        copy.wait()
    top_ref, kernel_ref, gain_row, bias_row, w_in_ref, b_in_row, w_out_ref, scale_row = held
    cotan_ref, taps_ref, gain_ref, bias_ref, scale_ref, b_in_ref, w_in_out, w_out_out, w_in_gain_ref, w_out_scale_ref = outs
    for row in range(ROWS):
        cotan_ref[:, block(row)] = top_ref[pl.ds(row, C, stride=ROWS), :]
    taps_ref[:, :TAPS] = kernel_ref[:, 0, :].T
    gain_ref[...] = column(gain_row[...])
    bias_ref[...] = column(bias_row[...])
    scale_ref[...] = column(scale_row[...])
    b_in_ref[...] = column(b_in_row[...])
    w_in_out[...] = w_in_ref[...]
    w_out_out[...] = w_out_ref[...]
    w_in_gain_ref[...] = w_in_ref[...] * gain_ref[...]
    w_out_scale_ref[...] = (w_out_ref[...] * scale_ref[...]).T


STRIP_AT = REACH * C
MESSAGE = (STRIP_AT + C, LANES)


def write_messages(field_ref, strip_ref, odd_ref, a_ref, b_ref):
    odd = odd_ref[0]
    for first, out_ref in (((1 - odd) * (ROWS - REACH), a_ref), (odd * (ROWS - REACH), b_ref)):
        for index in range(REACH):
            lanes = pl.ds(pl.multiple_of((first + index) * LANES, LANES), LANES)
            out_ref[pl.ds(index * C, C), :] = field_ref[:, lanes]
        out_ref[pl.ds(STRIP_AT, C), :] = strip_ref[...]


def outer_rows(group, a_ref, b_ref, odd):
    rows = {}
    for index in range(REACH + 1):
        at = pl.ds(index * C + group, GROUP)
        from_a, from_b = a_ref[at, :], b_ref[at, :]
        rows[index] = (jnp.where(odd, from_a, from_b), jnp.where(odd, from_b, from_a))
    above, below = rows.pop(REACH)
    found = {}
    for index in range(REACH):
        found[index - REACH] = with_edges(rows[index][0], above, ROWS - REACH + index)
        found[ROWS + index] = with_edges(rows[index][1], below, index)
    return found


def own_rows(channels, field_ref, strip_ref):
    strip = strip_ref[channels, :]
    return {row: with_edges(field_ref[channels, block(row)], strip, row) for row in range(ROWS)}


def edges(field_ref, left_ref, right_ref, odd_ref, strip_ref, a_ref, b_ref):
    strip_ref[...] = unfold(left_ref[...], right_ref[...], C // FOLD, FOLD)
    write_messages(field_ref, strip_ref, odd_ref, a_ref, b_ref)


def tap_index(a, b, flipped):
    tap = a * KS + b
    return TAPS - 1 - tap if flipped else tap


def conv_own(flipped, *refs):
    start_ref = refs[0] if flipped else None
    field_ref, strip_ref, taps_ref, out_ref = refs[-4:]
    lane = lane_of(GROUP)

    def conv_group(index, carry):
        channels = pl.ds(pl.multiple_of(index * GROUP, GROUP), GROUP)
        taps = taps_ref[channels, :]
        rows = own_rows(channels, field_ref, strip_ref)
        if flipped:
            sums = [start_ref[channels, block(row)] for row in range(ROWS)]
        else:
            sums = [jnp.zeros((GROUP, LANES), F32)] * ROWS
        for b in range(KS):
            moved = [shifted_row(*rows[row], lane, b - REACH) for row in range(ROWS)]
            for a in range(KS):
                weight = tap_of(taps, tap_index(a, b, flipped))
                for row in range(ROWS):
                    if 0 <= row + a - REACH < ROWS:
                        sums[row] = sums[row] + weight * moved[row + a - REACH]
        for row in range(ROWS):
            out_ref[channels, block(row)] = sums[row]
        return carry

    lax.fori_loop(0, C // GROUP, conv_group, 0)


def conv_edges(flipped, own_ref, a_ref, b_ref, odd_ref, taps_ref, put):
    odd = odd_ref[0] == 1
    lane = lane_of(GROUP)

    def conv_group(index, carry):
        group = pl.multiple_of(index * GROUP, GROUP)
        channels = pl.ds(group, GROUP)
        taps = taps_ref[channels, :]
        rows = outer_rows(group, a_ref, b_ref, odd)
        sums = [own_ref[channels, block(row)] for row in range(ROWS)]
        for b in range(KS):
            moved = {at: shifted_row(*row, lane, b - REACH) for at, row in rows.items()}
            for a in range(KS):
                if a == REACH:
                    continue
                weight = tap_of(taps, tap_index(a, b, flipped))
                for row in range(ROWS):
                    if row + a - REACH in moved:
                        sums[row] = sums[row] + weight * moved[row + a - REACH]
        put(group, sums)
        return carry

    lax.fori_loop(0, C // GROUP, conv_group, 0)


def forward(
    own_ref, a_ref, b_ref, odd_ref, taps_ref, gain_ref, bias_ref, w_in_ref, b_in_ref,
    normed_ref, inv_ref, slope_ref, hidden_ref,
):
    def put(group, sums):
        for row in range(ROWS):
            normed_ref[pl.ds(group, GROUP), block(row)] = sums[row]

    conv_edges(False, own_ref, a_ref, b_ref, odd_ref, taps_ref, put)
    w_in = split(w_in_ref[...])
    for start in range(0, CELLS, CHUNK):
        cells = pl.ds(start, CHUNK)
        conv_out = normed_ref[:, cells]
        centred = conv_out - jnp.mean(conv_out, axis=0, keepdims=True)
        inv = lax.rsqrt(jnp.mean(centred * centred, axis=0, keepdims=True) + EPSILON)
        normed = centred * inv
        normed_ref[:, cells] = normed
        inv_ref[:, cells] = inv
        lifted = normed * gain_ref[...] + bias_ref[...]
        pre_act = product(w_in, split(lifted), COL_COL) + b_in_ref[...]
        gate = 0.5 * (1.0 + lax.erf(pre_act * 0.7071067811865476))
        hidden_ref[:, cells] = pre_act * gate
        slope_ref[:, cells] = gate + pre_act * jnp.exp(-0.5 * pre_act * pre_act) * 0.3989422804014327


SAVED_SIDE = (HID // 4 + FOLD + GROUP, LANES)


def pack_saved(normed_ref, inv_ref, slope_ref, right_ref, left_ref):
    for edge, out_ref in ((LANES - REACH, right_ref), (0, left_ref)):
        at = 0
        for source_ref, rows, quarters in ((slope_ref, HID // 4, 4), (normed_ref, FOLD, 4), (inv_ref, 1, 1)):
            tall = max(rows, GROUP)
            lane = lane_of(tall)
            folded = jnp.zeros((tall, LANES), F32)
            for quarter in range(quarters):
                part = pl.ds(quarter * rows, rows)
                for row in range(ROWS):
                    to = 32 * quarter + REACH * row
                    value = jnp.broadcast_to(source_ref[part, block(row)], (tall, LANES))
                    folded = jnp.where((lane >= to) & (lane < to + REACH), roll(value, to - edge), folded)
            out_ref[pl.ds(at, tall), :] = folded
            at += tall


def unpack_saved(left_ref, right_ref, normed_ref, inv_ref, slope_ref):
    at = 0
    for out_ref, rows, quarters in ((slope_ref, HID // 4, 4), (normed_ref, FOLD, 4), (inv_ref, GROUP, 1)):
        part = pl.ds(at, rows)
        out_ref[...] = unfold(left_ref[part, :], right_ref[part, :], quarters, rows)
        at += rows


def grad_at(cotan, w_out, w_in, normed, inv, slope):
    grad_pre = product(w_out, split(cotan), ROW_COL) * slope
    grad_normed = product(w_in, split(grad_pre), ROW_COL)
    mean = jnp.mean(grad_normed, axis=0, keepdims=True)
    along = jnp.mean(grad_normed * normed, axis=0, keepdims=True)
    return grad_pre, inv * (grad_normed - mean - normed * along)


def step_tile(cotan_refs, saved, grad_ref, keep):
    normed_ref, inv_ref, slope_ref, w_in_gain_ref, w_out_scale_ref = saved
    w_out = split(w_out_scale_ref[...])
    w_in = split(w_in_gain_ref[...])
    for start in range(0, CELLS, CHUNK):
        cells = pl.ds(start, CHUNK)
        cotan = sum(ref[:, cells] for ref in cotan_refs)
        grad_pre, grad = grad_at(cotan, w_out, w_in, normed_ref[:, cells], inv_ref[:, cells], slope_ref[:, cells])
        keep(cells, cotan, grad_pre)
        grad_ref[:, cells] = grad
    return w_out, w_in


def ignore(cells, cotan, grad_pre):
    pass


def first_step(cotan_ref, *refs):
    saved, (grad_ref, right_ref, left_ref) = refs[:5], refs[5:]
    step_tile((cotan_ref,), saved, grad_ref, ignore)
    pack_edges(grad_ref, right_ref, left_ref)


def step_sides(lefts, rights, weights, strips):
    left, right = sum(ref[...] for ref in lefts), sum(ref[...] for ref in rights)
    normed_ref, inv_ref, slope_ref = strips
    cotan = unfold(left, right, C // FOLD, FOLD)
    return grad_at(cotan, *weights, normed_ref[...], inv_ref[:1, :], slope_ref[...])[1]


def middle_step(cotan_ref, from_left, from_right, odd_ref, *refs):
    saved, strips, (grad_ref, strip_ref, a_ref, b_ref) = refs[:5], refs[5:8], refs[8:]
    weights = step_tile((cotan_ref,), saved, grad_ref, ignore)
    strip_ref[...] = step_sides((from_left,), (from_right,), weights, strips)
    write_messages(grad_ref, strip_ref, odd_ref, a_ref, b_ref)


def last_step(count, *refs):
    cotans, lefts, rights = refs[:count], refs[count : 2 * count - 1], refs[2 * count - 1 : 3 * count - 2]
    first_strip, odd_ref = refs[3 * count - 2 : 3 * count]
    refs = refs[3 * count :]
    saved, strips = refs[:5], refs[5:8]
    grad_ref, strip_ref, a_ref, b_ref, cotan_ref, grad_pre_ref = refs[8:]

    def keep(cells, cotan, grad_pre):
        cotan_ref[:, cells] = cotan
        grad_pre_ref[:, cells] = grad_pre

    weights = step_tile(cotans, saved, grad_ref, keep)
    strip_ref[...] = step_sides(lefts, rights, weights, strips) + first_strip[...]
    write_messages(grad_ref, strip_ref, odd_ref, a_ref, b_ref)


def finish(own_ref, a_ref, b_ref, odd_ref, taps_ref, out_ref, right_ref, left_ref):
    def put(group, sums):
        for row in range(ROWS):
            out_ref[pl.ds(group, GROUP), block(row)] = sums[row]

    conv_edges(True, own_ref, a_ref, b_ref, odd_ref, taps_ref, put)
    pack_edges(out_ref, right_ref, left_ref)


def last_finish(own_ref, a_ref, b_ref, odd_ref, taps_ref, out_ref):
    def put(group, sums):
        for row in range(ROWS):
            out_ref[pl.ds(group * ROWS + row, GROUP, stride=ROWS), :] = sums[row]

    conv_edges(True, own_ref, a_ref, b_ref, odd_ref, taps_ref, put)


LIFT_ROWS = C + GROUP
OUT_AT = 0
IN_AT = OUT_AT + C * HID // LANES
TAPS_AT = IN_AT + LIFT_ROWS * HID // LANES
USED_ROWS = TAPS_AT + C


def parameter_terms(
    field_ref, strip_ref, a_ref, b_ref, odd_ref, grad_ref, cotan_ref, hidden_ref, normed_ref, grad_pre_ref,
    payload_ref,
):
    odd = odd_ref[0] == 1
    lane = lane_of(GROUP)

    def taps_group(index, carry):
        group = pl.multiple_of(index * GROUP, GROUP)
        found = outer_rows(group, a_ref, b_ref, odd) | own_rows(pl.ds(group, GROUP), field_ref, strip_ref)
        rows = [found[row] for row in sorted(found)]
        grads = [grad_ref[pl.ds(group, GROUP), block(row)] for row in range(ROWS)]
        result = jnp.zeros((GROUP, LANES), F32)
        for b in range(KS):
            moved = [shifted_row(*row, lane, b - REACH) for row in rows]
            for a in range(KS):
                terms = [grads[row] * moved[row + a] for row in range(ROWS)]
                while len(terms) > 1:
                    terms = [one + two for one, two in zip(terms[0::2], terms[1::2])]
                total = jnp.sum(terms[0], axis=1, keepdims=True)
                result = jnp.where(lane == a * KS + b, total, result)
        payload_ref[pl.ds(TAPS_AT + group, GROUP), :] = result
        return carry

    lax.fori_loop(0, C // GROUP, taps_group, 0)
    grad_w_out = product(split(cotan_ref[...]), split(hidden_ref[...]), ROW_ROW)
    ones = jnp.where(lax.broadcasted_iota(jnp.int32, (GROUP, CELLS), 0) == 0, 1.0, 0.0)
    lifted = jnp.concatenate([normed_ref[...], ones], axis=0)
    grad_w_in = product(split(lifted), split(grad_pre_ref[...]), ROW_ROW)
    for part in range(HID // LANES):
        payload_ref[pl.ds(OUT_AT + part * C, C), :] = grad_w_out[:, part * LANES : (part + 1) * LANES]
        payload_ref[pl.ds(IN_AT + part * LIFT_ROWS, LIFT_ROWS), :] = grad_w_in[:, part * LANES : (part + 1) * LANES]
    payload_ref[pl.ds(USED_ROWS, PAYLOAD_ROWS - USED_ROWS), :] = jnp.zeros((PAYLOAD_ROWS - USED_ROWS, LANES), F32)


def sum_shares(shares_ref, out_ref):
    devices, rows = out_ref.shape[0], out_ref.shape[1]

    def add(device, total):
        return total + shares_ref[device]

    total = lax.fori_loop(1, devices, add, shares_ref[0], unroll=7)

    def put(device, carry):
        out_ref[device] = total
        return carry

    lax.fori_loop(0, devices, put, 0, unroll=8)


def parameter_grads(
    payload_ref, gain_ref, bias_ref, w_in_ref, w_out_ref, scale_ref,
    kernel_out, gain_out, bias_out, w_in_out, b_in_out, w_out_out, scale_out,
):
    kernel_out[:, 0, :] = payload_ref[pl.ds(TAPS_AT, C), :].T[:TAPS, :]
    scale = scale_ref[...]
    sums = [jnp.zeros((C, 1), F32)] * 3
    for part in range(HID // LANES):
        hidden = pl.ds(part * LANES, LANES)
        grad_out = payload_ref[pl.ds(OUT_AT + part * C, C), :]
        w_out_out[:, hidden] = grad_out * scale
        at = IN_AT + part * LIFT_ROWS
        grad_in = payload_ref[pl.ds(at, C), :]
        grad_b = payload_ref[pl.ds(at + C, 1), :]
        b_in_out[:, hidden] = grad_b
        w_in_out[:, hidden] = grad_in * gain_ref[...] + bias_ref[...] * grad_b
        w_in = w_in_ref[:, hidden]
        terms = (w_in * grad_in, w_in * grad_b, w_out_ref[:, hidden] * grad_out)
        sums = [total + jnp.sum(term, axis=1, keepdims=True) for total, term in zip(sums, terms)]
    for total, out in zip(sums, (gain_out, bias_out, scale_out)):
        out[...] = jnp.broadcast_to(total, (C, LANES)).T[:1, :]


def pairs(axis, sections, odd_pairs):
    size = lax.axis_size(axis)
    routes = []
    for section in sections:
        for tile in range(1 if odd_pairs else 0, size - 1, 2):
            here = section * size + tile
            routes += [(here, here + 1), (here + 1, here)]
    return routes


def swap_rows(message_a, message_b, sections):
    axes = ("section", "ty")
    return (
        lax.ppermute(message_a, axes, pairs("ty", sections, False)),
        lax.ppermute(message_b, axes, pairs("ty", sections, True)),
    )


def to_sides(to_right, to_left, sections, back=0):
    size = lax.axis_size("tx")
    right = [(s * size + i, (s - back) * size + i + 1) for s in sections for i in range(size - 1)]
    left = [(s * size + i + 1, (s - back) * size + i) for s in sections for i in range(size - 1)]
    axes = ("section", "tx")
    return lax.ppermute(to_right, axes, right), lax.ppermute(to_left, axes, left)


def sum_over_tiles(payload):
    devices = lax.axis_size(TILES)
    rows = PAYLOAD_ROWS // devices
    shares = lax.all_to_all(payload.reshape(devices, rows, LANES), TILES, 0, 0)
    (copies,) = call(sum_shares, [(devices, rows, LANES)], shares)
    return lax.all_to_all(copies, TILES, 0, 0).reshape(PAYLOAD_ROWS, LANES)


def on_device(acts, top_grad, kernel, ln_gain, ln_bias, w_in, b_in, w_out, layer_scale):
    sections = lax.axis_size("section")
    every = range(sections)
    is_last = (lax.axis_index("section") == sections - 1).astype(F32)
    odd = lax.rem(lax.axis_index("ty"), 2).astype(jnp.int32).reshape(1)
    field_shape, side, wide, hidden_shape = ((C, CELLS), (FOLD, LANES), (C, LANES), (HID, CELLS))
    edge_outs = [wide, MESSAGE, MESSAGE]
    acts_rows, top_rows = (acts.reshape(C * ROWS, LANES), top_grad.reshape(C * ROWS, LANES))

    field, to_right, to_left = call(take_field, [field_shape, side, side], acts_rows)
    left, right = to_sides(to_right, to_left, every)
    parameters = (
        top_rows, jnp.transpose(kernel, (1, 0, 2)), ln_gain, ln_bias, w_in[0], b_in, w_out[0].T, layer_scale,
    )
    cotan, taps, gain, shift_bias, scale, bias_in, weight_in, weight_out, w_in_gain, w_out_scale = call(
        prepare,
        [field_shape, wide, (C, 1), (C, 1), (C, 1), (HID, 1), (C, HID), (C, HID), (C, HID), (HID, C)],
        *parameters, scratch=[p.shape for p in parameters] + [pltpu.SemaphoreType.DMA((len(parameters),))], copied=True,
    )
    strip, message_a, message_b = call(edges, edge_outs, field, left, right, odd)
    from_a, from_b = swap_rows(message_a, message_b, every)
    (own,) = call(functools.partial(conv_own, False), [field_shape], field, strip, taps, flops=CONV_FLOPS)
    around = (field, strip, from_a, from_b, odd)
    normed, inv, slope, hidden = call(
        forward,
        [field_shape, (1, CELLS), hidden_shape, hidden_shape],
        own, from_a, from_b, odd, taps, gain, shift_bias, weight_in, bias_in,
    )
    saved = (normed, inv, slope, w_in_gain, w_out_scale)

    cotan = cotan * is_last
    cotans, lefts, rights = [cotan], [], []
    strips = ()
    for section in reversed(every):
        only = (section,) if section else every
        if section == sections - 1:
            grad, to_right, to_left = call(first_step, [field_shape, side, side], cotan, *saved)
            grad_left, grad_right = to_sides(to_right, to_left, only)
            tile, grad = lax.optimization_barrier((saved[:3], grad))
            saved_right, saved_left = call(pack_saved, [SAVED_SIDE, SAVED_SIDE], *tile)
            grad_left, saved_right, saved_left = lax.optimization_barrier((grad_left, saved_right, saved_left))
            saved_sides = to_sides(saved_right, saved_left, range(sections - 1))
            first_strip, message_a, message_b = call(edges, edge_outs, grad, grad_left, grad_right, odd)
            grad_strip = first_strip
            strips = call(unpack_saved, [wide, (GROUP, LANES), (HID, LANES)], *saved_sides)
        elif section:
            grad, grad_strip, message_a, message_b = call(
                middle_step, [field_shape] + edge_outs, cotan, lefts[-1], rights[-1], odd, *saved, *strips
            )
        else:
            grad, grad_strip, message_a, message_b, cotan, grad_pre = call(
                functools.partial(last_step, len(cotans)), [field_shape] + edge_outs + [field_shape, hidden_shape],
                *cotans, *lefts, *rights, first_strip, odd, *saved, *strips,
            )
            (payload,) = call(
                parameter_terms, [(PAYLOAD_ROWS, LANES)],
                *around, grad, cotan, hidden, normed, grad_pre, flops=4 * CONV_FLOPS,
            )
        grad_a, grad_b = swap_rows(message_a, message_b, only)
        (own,) = call(
            functools.partial(conv_own, True), [field_shape], cotan, grad, grad_strip, taps, flops=CONV_FLOPS
        )
        if section:
            cotan, to_right, to_left = call(finish, [field_shape, side, side], own, grad_a, grad_b, odd, taps)
            cotan = lax.ppermute(cotan, "section", [(section, section - 1)])
            from_left, from_right = to_sides(to_right, to_left, only, 1)
            cotans.append(cotan)
            lefts.append(from_left)
            rights.append(from_right)
    (input_grad,) = call(last_finish, [(C * ROWS, LANES)], own, grad_a, grad_b, odd, taps)
    payload = sum_over_tiles(payload)
    grad_kernel, grad_gain, grad_bias, grad_w_in, grad_b_in, grad_w_out, grad_scale = call(
        parameter_grads,
        [(TAPS, 1, C), (1, C), (1, C), (C, HID), (1, HID), (C, HID), (1, C)],
        payload, gain, shift_bias, weight_in, weight_out, scale,
    )
    return (
        input_grad.reshape(1, 1, C, ROWS, LANES),
        jnp.transpose(grad_kernel, (1, 0, 2)),
        grad_gain,
        grad_bias,
        grad_w_in[None],
        grad_b_in,
        grad_w_out.T[None],
        grad_scale,
    )


def solution(mesh):
    placed = (
        P("section", None, None, "ty", "tx"),
        P(None, None, "ty", "tx"),
        P("section", None, None),
        P("section", None),
        P("section", None),
        P("section", None, None),
        P("section", None),
        P("section", None, None),
        P("section", None),
    )
    return jax.shard_map(
        on_device,
        mesh=mesh,
        in_specs=placed,
        out_specs=(
            P("section", None, None, "ty", "tx"),
            P("section", None, None),
            P("section", None),
            P("section", None),
            P("section", None, None),
            P("section", None),
            P("section", None, None),
            P("section", None),
        ),
        check_vma=False,
    )
```

```python
import functools

import jax
import jax.numpy as jnp
from jax import lax
from jax.experimental import pallas as pl
from jax.experimental.pallas import tpu as pltpu
from jax.sharding import PartitionSpec as P

KS = 7
TAPS = KS * KS
REACH = KS // 2
EPSILON = 1e-06
LANES = 128
GROUP = 8
ROWS = 8
C = 96
HID = 384
CELLS = ROWS * LANES
FOLD = 24
CHUNK = 256
PAYLOAD_ROWS = 1024
F32 = jnp.float32
BF16 = jnp.bfloat16
CONV_FLOPS = 2 * TAPS * C * CELLS
TILES = ("ty", "tx")


def call(kernel, outs, *operands, scratch=(), flops=0, copied=False):
    whole = pl.BlockSpec(memory_space=pltpu.VMEM)
    specs = [
        pl.BlockSpec(memory_space=pltpu.SMEM if operand.dtype == jnp.int32 else pltpu.HBM if copied else pltpu.VMEM)
        for operand in operands
    ]
    spaces = [pltpu.VMEM(shape, F32) if isinstance(shape, tuple) else shape for shape in scratch]
    return pl.pallas_call(
        kernel,
        out_shape=[jax.ShapeDtypeStruct(shape, F32) for shape in outs],
        in_specs=specs,
        out_specs=[whole] * len(outs),
        scratch_shapes=spaces,
        compiler_params=pltpu.CompilerParams(vmem_limit_bytes=28 * 1024 * 1024),
        cost_estimate=pl.CostEstimate(flops=flops, bytes_accessed=0, transcendentals=0) if flops else None,
    )(*operands)


def roll(value, shift):
    return pltpu.roll(value, shift % LANES, 1)


def lane_of(rows):
    return lax.broadcasted_iota(jnp.int32, (rows, LANES), 1)


def block(row):
    return pl.ds(row * LANES, LANES)


def split(value):
    high = value.astype(BF16)
    low = (value - high.astype(F32)).astype(BF16)
    return high, low


def product(left, right, dims):
    def part(one, two):
        return lax.dot_general(one, two, (dims, ((), ())), preferred_element_type=F32)

    return part(left[0], right[0]) + (part(left[0], right[1]) + part(left[1], right[0]))


ROW_COL = ((1,), (0,))
COL_COL = ((0,), (0,))
ROW_ROW = ((1,), (1,))


def pack_edges(field_ref, right_ref, left_ref):
    lane = lane_of(FOLD)
    for edge, out_ref in ((LANES - REACH, right_ref), (0, left_ref)):
        folded = jnp.zeros((FOLD, LANES), F32)
        for quarter in range(C // FOLD):
            part = pl.ds(quarter * FOLD, FOLD)
            for row in range(ROWS):
                at = 32 * quarter + REACH * row
                moved = roll(field_ref[part, block(row)], at - edge)
                folded = jnp.where((lane >= at) & (lane < at + REACH), moved, folded)
        out_ref[...] = folded


SIDE = 32


def unfold(left, right, quarters, rows):
    lane = lane_of(rows)
    parts = []
    for quarter in range(quarters):
        theirs = roll(left, -32 * quarter)
        parts.append(jnp.where(lane < SIDE, theirs, jnp.where(lane < 2 * SIDE, roll(right, SIDE - 32 * quarter), 0.0)))
    return jnp.concatenate(parts, axis=0)


def shifted_row(row, left, right, lane, distance):
    if distance > 0:
        return roll(jnp.where(lane < distance, right, row), -distance)
    if distance < 0:
        return roll(jnp.where(lane >= LANES + distance, left, row), -distance)
    return row


def with_edges(value, strip, row):
    return value, roll(strip, LANES - REACH - REACH * row), roll(strip, -SIDE - REACH * row)


def tap_of(taps_ref, tap, group):
    return taps_ref[pl.ds(tap * C + group, GROUP), :]


def take_field(acts_ref, field_ref, right_ref, left_ref):
    for row in range(ROWS):
        field_ref[:, block(row)] = acts_ref[pl.ds(row, C, stride=ROWS), :]
    pack_edges(field_ref, right_ref, left_ref)


def column(row):
    return jnp.broadcast_to(row, (GROUP, row.shape[1])).T[:, :1]


def prepare(*refs):
    count = 8
    sources, outs, held = refs[: count], refs[count : -count - 1], refs[-count - 1 : -1]
    sems = refs[-1]
    copies = [pltpu.make_async_copy(source, target, sems.at[i]) for i, (source, target) in enumerate(zip(sources, held))]
    for copy in copies:
        copy.start()
    for copy in copies:
        copy.wait()
    top_ref, kernel_ref, gain_row, bias_row, w_in_ref, b_in_row, w_out_ref, scale_row = held
    cotan_ref, taps_ref, gain_ref, bias_ref, scale_ref, b_in_ref, w_in_out, w_out_out, w_in_gain_ref, w_out_scale_ref = outs
    for row in range(ROWS):
        cotan_ref[:, block(row)] = top_ref[pl.ds(row, C, stride=ROWS), :]
    taps = kernel_ref[:, 0, :].T
    for tap in range(TAPS):
        taps_ref[pl.ds(tap * C, C), :] = jnp.broadcast_to(taps[:, tap : tap + 1], (C, LANES))
    gain_ref[...] = column(gain_row[...])
    bias_ref[...] = column(bias_row[...])
    scale_ref[...] = column(scale_row[...])
    b_in_ref[...] = column(b_in_row[...])
    w_in_out[...] = w_in_ref[...]
    w_out_out[...] = w_out_ref[...]
    w_in_gain_ref[...] = w_in_ref[...] * gain_ref[...]
    w_out_scale_ref[...] = (w_out_ref[...] * scale_ref[...]).T


STRIP_AT = REACH * C
MESSAGE = (STRIP_AT + C, LANES)


def write_messages(field_ref, strip_ref, odd_ref, a_ref, b_ref):
    odd = odd_ref[0]
    for first, out_ref in (((1 - odd) * (ROWS - REACH), a_ref), (odd * (ROWS - REACH), b_ref)):
        for index in range(REACH):
            lanes = pl.ds(pl.multiple_of((first + index) * LANES, LANES), LANES)
            out_ref[pl.ds(index * C, C), :] = field_ref[:, lanes]
        out_ref[pl.ds(STRIP_AT, C), :] = strip_ref[...]


def outer_rows(group, a_ref, b_ref, odd):
    rows = {}
    for index in range(REACH + 1):
        at = pl.ds(index * C + group, GROUP)
        from_a, from_b = a_ref[at, :], b_ref[at, :]
        rows[index] = (jnp.where(odd, from_a, from_b), jnp.where(odd, from_b, from_a))
    above, below = rows.pop(REACH)
    found = {}
    for index in range(REACH):
        found[index - REACH] = with_edges(rows[index][0], above, ROWS - REACH + index)
        found[ROWS + index] = with_edges(rows[index][1], below, index)
    return found


def own_rows(channels, field_ref, strip_ref):
    strip = strip_ref[channels, :]
    return {row: with_edges(field_ref[channels, block(row)], strip, row) for row in range(ROWS)}


def edges(field_ref, left_ref, right_ref, odd_ref, strip_ref, a_ref, b_ref):
    strip_ref[...] = unfold(left_ref[...], right_ref[...], C // FOLD, FOLD)
    write_messages(field_ref, strip_ref, odd_ref, a_ref, b_ref)


def tap_index(a, b, flipped):
    tap = a * KS + b
    return TAPS - 1 - tap if flipped else tap


def conv_own(flipped, *refs):
    start_ref = refs[0] if flipped else None
    field_ref, strip_ref, taps_ref, out_ref = refs[-4:]
    lane = lane_of(GROUP)

    def conv_group(index, carry):
        group = pl.multiple_of(index * GROUP, GROUP)
        channels = pl.ds(group, GROUP)
        rows = own_rows(channels, field_ref, strip_ref)
        if flipped:
            sums = [start_ref[channels, block(row)] for row in range(ROWS)]
        else:
            sums = [jnp.zeros((GROUP, LANES), F32)] * ROWS
        for b in range(KS):
            moved = [shifted_row(*rows[row], lane, b - REACH) for row in range(ROWS)]
            for a in range(KS):
                weight = tap_of(taps_ref, tap_index(a, b, flipped), group)
                for row in range(ROWS):
                    if 0 <= row + a - REACH < ROWS:
                        sums[row] = sums[row] + weight * moved[row + a - REACH]
        for row in range(ROWS):
            out_ref[channels, block(row)] = sums[row]
        return carry

    lax.fori_loop(0, C // GROUP, conv_group, 0)


def conv_edges(flipped, own_ref, a_ref, b_ref, odd_ref, taps_ref, put):
    odd = odd_ref[0] == 1
    lane = lane_of(GROUP)

    def conv_group(index, carry):
        group = pl.multiple_of(index * GROUP, GROUP)
        channels = pl.ds(group, GROUP)
        rows = outer_rows(group, a_ref, b_ref, odd)
        sums = [own_ref[channels, block(row)] for row in range(ROWS)]
        for b in range(KS):
            moved = {at: shifted_row(*row, lane, b - REACH) for at, row in rows.items()}
            for a in range(KS):
                if a == REACH:
                    continue
                weight = tap_of(taps_ref, tap_index(a, b, flipped), group)
                for row in range(ROWS):
                    if row + a - REACH in moved:
                        sums[row] = sums[row] + weight * moved[row + a - REACH]
        put(group, sums)
        return carry

    lax.fori_loop(0, C // GROUP, conv_group, 0)


def forward(
    own_ref, a_ref, b_ref, odd_ref, taps_ref, gain_ref, bias_ref, w_in_ref, b_in_ref,
    normed_ref, inv_ref, slope_ref, hidden_ref,
):
    def put(group, sums):
        for row in range(ROWS):
            normed_ref[pl.ds(group, GROUP), block(row)] = sums[row]

    conv_edges(False, own_ref, a_ref, b_ref, odd_ref, taps_ref, put)
    w_in = split(w_in_ref[...])
    for start in range(0, CELLS, CHUNK):
        cells = pl.ds(start, CHUNK)
        conv_out = normed_ref[:, cells]
        centred = conv_out - jnp.mean(conv_out, axis=0, keepdims=True)
        inv = lax.rsqrt(jnp.mean(centred * centred, axis=0, keepdims=True) + EPSILON)
        normed = centred * inv
        normed_ref[:, cells] = normed
        inv_ref[:, cells] = inv
        lifted = normed * gain_ref[...] + bias_ref[...]
        pre_act = product(w_in, split(lifted), COL_COL) + b_in_ref[...]
        gate = 0.5 * (1.0 + lax.erf(pre_act * 0.7071067811865476))
        hidden_ref[:, cells] = pre_act * gate
        slope_ref[:, cells] = gate + pre_act * jnp.exp(-0.5 * pre_act * pre_act) * 0.3989422804014327


SAVED_SIDE = (HID // 4 + FOLD + GROUP, LANES)


def pack_saved(normed_ref, inv_ref, slope_ref, right_ref, left_ref):
    for edge, out_ref in ((LANES - REACH, right_ref), (0, left_ref)):
        at = 0
        for source_ref, rows, quarters in ((slope_ref, HID // 4, 4), (normed_ref, FOLD, 4), (inv_ref, 1, 1)):
            tall = max(rows, GROUP)
            lane = lane_of(tall)
            folded = jnp.zeros((tall, LANES), F32)
            for quarter in range(quarters):
                part = pl.ds(quarter * rows, rows)
                for row in range(ROWS):
                    to = 32 * quarter + REACH * row
                    value = jnp.broadcast_to(source_ref[part, block(row)], (tall, LANES))
                    folded = jnp.where((lane >= to) & (lane < to + REACH), roll(value, to - edge), folded)
            out_ref[pl.ds(at, tall), :] = folded
            at += tall


def unpack_saved(left_ref, right_ref, normed_ref, inv_ref, slope_ref):
    at = 0
    for out_ref, rows, quarters in ((slope_ref, HID // 4, 4), (normed_ref, FOLD, 4), (inv_ref, GROUP, 1)):
        part = pl.ds(at, rows)
        out_ref[...] = unfold(left_ref[part, :], right_ref[part, :], quarters, rows)
        at += rows


def grad_at(cotan, w_out, w_in, normed, inv, slope):
    grad_pre = product(w_out, split(cotan), ROW_COL) * slope
    grad_normed = product(w_in, split(grad_pre), ROW_COL)
    mean = jnp.mean(grad_normed, axis=0, keepdims=True)
    along = jnp.mean(grad_normed * normed, axis=0, keepdims=True)
    return grad_pre, inv * (grad_normed - mean - normed * along)


def step_tile(cotan_refs, saved, grad_ref, keep):
    normed_ref, inv_ref, slope_ref, w_in_gain_ref, w_out_scale_ref = saved
    w_out = split(w_out_scale_ref[...])
    w_in = split(w_in_gain_ref[...])
    for start in range(0, CELLS, CHUNK):
        cells = pl.ds(start, CHUNK)
        cotan = sum(ref[:, cells] for ref in cotan_refs)
        grad_pre, grad = grad_at(cotan, w_out, w_in, normed_ref[:, cells], inv_ref[:, cells], slope_ref[:, cells])
        keep(cells, cotan, grad_pre)
        grad_ref[:, cells] = grad
    return w_out, w_in


def ignore(cells, cotan, grad_pre):
    pass


def first_step(cotan_ref, *refs):
    saved, (grad_ref, right_ref, left_ref) = refs[:5], refs[5:]
    step_tile((cotan_ref,), saved, grad_ref, ignore)
    pack_edges(grad_ref, right_ref, left_ref)


def step_sides(lefts, rights, weights, strips):
    left, right = sum(ref[...] for ref in lefts), sum(ref[...] for ref in rights)
    normed_ref, inv_ref, slope_ref = strips
    cotan = unfold(left, right, C // FOLD, FOLD)
    return grad_at(cotan, *weights, normed_ref[...], inv_ref[:1, :], slope_ref[...])[1]


def middle_step(cotan_ref, from_left, from_right, odd_ref, *refs):
    saved, strips, (grad_ref, strip_ref, a_ref, b_ref) = refs[:5], refs[5:8], refs[8:]
    weights = step_tile((cotan_ref,), saved, grad_ref, ignore)
    strip_ref[...] = step_sides((from_left,), (from_right,), weights, strips)
    write_messages(grad_ref, strip_ref, odd_ref, a_ref, b_ref)


def last_step(count, *refs):
    cotans, lefts, rights = refs[:count], refs[count : 2 * count - 1], refs[2 * count - 1 : 3 * count - 2]
    first_strip, odd_ref = refs[3 * count - 2 : 3 * count]
    refs = refs[3 * count :]
    saved, strips = refs[:5], refs[5:8]
    grad_ref, strip_ref, a_ref, b_ref, cotan_ref, grad_pre_ref = refs[8:]

    def keep(cells, cotan, grad_pre):
        cotan_ref[:, cells] = cotan
        grad_pre_ref[:, cells] = grad_pre

    weights = step_tile(cotans, saved, grad_ref, keep)
    strip_ref[...] = step_sides(lefts, rights, weights, strips) + first_strip[...]
    write_messages(grad_ref, strip_ref, odd_ref, a_ref, b_ref)


def finish(own_ref, a_ref, b_ref, odd_ref, taps_ref, out_ref, right_ref, left_ref):
    def put(group, sums):
        for row in range(ROWS):
            out_ref[pl.ds(group, GROUP), block(row)] = sums[row]

    conv_edges(True, own_ref, a_ref, b_ref, odd_ref, taps_ref, put)
    pack_edges(out_ref, right_ref, left_ref)


def last_finish(own_ref, a_ref, b_ref, odd_ref, taps_ref, out_ref):
    def put(group, sums):
        for row in range(ROWS):
            out_ref[pl.ds(group * ROWS + row, GROUP, stride=ROWS), :] = sums[row]

    conv_edges(True, own_ref, a_ref, b_ref, odd_ref, taps_ref, put)


LIFT_ROWS = C + GROUP
OUT_AT = 0
IN_AT = OUT_AT + C * HID // LANES
TAPS_AT = IN_AT + LIFT_ROWS * HID // LANES
USED_ROWS = TAPS_AT + C


HALF = PAYLOAD_ROWS // 2


def half_of(odd):
    return pl.ds(pl.multiple_of(odd * HALF, HALF), HALF)


def parameter_terms(
    field_ref, strip_ref, a_ref, b_ref, odd_ref, grad_ref, cotan_ref, hidden_ref, normed_ref, grad_pre_ref,
    gain_ref, bias_ref, scale_ref, w_in_ref, w_out_ref,
    mine_ref, theirs_ref, payload_ref,
):
    odd = odd_ref[0] == 1
    lane = lane_of(GROUP)

    def taps_group(index, carry):
        group = pl.multiple_of(index * GROUP, GROUP)
        found = outer_rows(group, a_ref, b_ref, odd) | own_rows(pl.ds(group, GROUP), field_ref, strip_ref)
        rows = [found[row] for row in sorted(found)]
        grads = [grad_ref[pl.ds(group, GROUP), block(row)] for row in range(ROWS)]
        result = jnp.zeros((GROUP, LANES), F32)
        for b in range(KS):
            moved = [shifted_row(*row, lane, b - REACH) for row in rows]
            for a in range(KS):
                terms = [grads[row] * moved[row + a] for row in range(ROWS)]
                while len(terms) > 1:
                    terms = [one + two for one, two in zip(terms[0::2], terms[1::2])]
                total = jnp.sum(terms[0], axis=1, keepdims=True)
                result = jnp.where(lane == a * KS + b, total, result)
        payload_ref[pl.ds(TAPS_AT + group, GROUP), :] = result
        return carry

    lax.fori_loop(0, C // GROUP, taps_group, 0)
    grad_w_out = product(split(cotan_ref[...]), split(hidden_ref[...]), ROW_ROW)
    ones = jnp.where(lax.broadcasted_iota(jnp.int32, (GROUP, CELLS), 0) == 0, 1.0, 0.0)
    lifted = jnp.concatenate([normed_ref[...], ones], axis=0)
    grad_w_in = product(split(lifted), split(grad_pre_ref[...]), ROW_ROW)
    grad_b_in = grad_w_in[C : C + 1, :]
    columns = (w_in_ref[...] * grad_w_in[:C, :], w_in_ref[...] * grad_b_in, w_out_ref[...] * grad_w_out)
    lane = lane_of(C)
    for index, terms in enumerate(columns):
        total = jnp.sum(terms, axis=1, keepdims=True)
        taps = payload_ref[pl.ds(TAPS_AT, C), :]
        payload_ref[pl.ds(TAPS_AT, C), :] = jnp.where(lane == TAPS + index, total, taps)
    grad_w_out = grad_w_out * scale_ref[...]
    grad_weights = grad_w_in[:C, :] * gain_ref[...] + bias_ref[...] * grad_b_in
    for part in range(HID // LANES):
        lanes = slice(part * LANES, (part + 1) * LANES)
        at = IN_AT + part * LIFT_ROWS
        payload_ref[pl.ds(OUT_AT + part * C, C), :] = grad_w_out[:, lanes]
        payload_ref[pl.ds(at, C), :] = grad_weights[:, lanes]
        payload_ref[pl.ds(at + C, GROUP), :] = grad_w_in[C:, lanes]
    payload_ref[pl.ds(USED_ROWS, PAYLOAD_ROWS - USED_ROWS), :] = jnp.zeros((PAYLOAD_ROWS - USED_ROWS, LANES), F32)
    mine_ref[...] = payload_ref[half_of(odd_ref[0]), :]
    theirs_ref[...] = payload_ref[half_of(1 - odd_ref[0]), :]


def sum_shares(shares_ref, out_ref):
    devices = out_ref.shape[0]
    terms = [shares_ref[device] for device in range(devices)]
    while len(terms) > 1:
        terms = [one + two for one, two in zip(terms[0::2], terms[1::2])]
    for device in range(devices):
        out_ref[device] = terms[0]


def parameter_grads(
    mine_ref, theirs_ref, odd_ref,
    kernel_out, gain_out, bias_out, w_in_out, b_in_out, w_out_out, scale_out,
    payload_ref,
):
    payload_ref[half_of(odd_ref[0]), :] = mine_ref[...]
    payload_ref[half_of(1 - odd_ref[0]), :] = theirs_ref[...]
    by_tap = payload_ref[pl.ds(TAPS_AT, C), :].T
    kernel_out[:, 0, :] = by_tap[:TAPS, :]
    for index, out_ref in enumerate((gain_out, bias_out, scale_out)):
        out_ref[...] = by_tap[TAPS + index : TAPS + index + 1, :]
    for part in range(HID // LANES):
        hidden = pl.ds(part * LANES, LANES)
        at = IN_AT + part * LIFT_ROWS
        w_out_out[:, hidden] = payload_ref[pl.ds(OUT_AT + part * C, C), :]
        w_in_out[:, hidden] = payload_ref[pl.ds(at, C), :]
        b_in_out[:, hidden] = payload_ref[pl.ds(at + C, 1), :]


def pairs(axis, sections, odd_pairs):
    size = lax.axis_size(axis)
    routes = []
    for section in sections:
        for tile in range(1 if odd_pairs else 0, size - 1, 2):
            here = section * size + tile
            routes += [(here, here + 1), (here + 1, here)]
    return routes


def swap_rows(message_a, message_b, sections):
    axes = ("section", "ty")
    return (
        lax.ppermute(message_a, axes, pairs("ty", sections, False)),
        lax.ppermute(message_b, axes, pairs("ty", sections, True)),
    )


def to_sides(to_right, to_left, sections, back=0):
    size = lax.axis_size("tx")
    right = [(s * size + i, (s - back) * size + i + 1) for s in sections for i in range(size - 1)]
    left = [(s * size + i + 1, (s - back) * size + i) for s in sections for i in range(size - 1)]
    axes = ("section", "tx")
    return lax.ppermute(to_right, axes, right), lax.ppermute(to_left, axes, left)


def swap_pairs(half):
    return lax.ppermute(half, "ty", [(tile, tile ^ 1) for tile in range(lax.axis_size("ty"))])


def sum_over_tiles(mine, theirs, beside):
    columns = lax.axis_size("tx")
    tiles = lax.axis_size("ty")
    groups = [[tile * columns + i for tile in range(odd, tiles, 2) for i in range(columns)] for odd in range(2)]
    devices = len(groups[0])

    def to_all(shares):
        return lax.all_to_all(shares, TILES, 0, 0, axis_index_groups=groups)

    half = mine + swap_pairs(theirs)
    shares = to_all(half.reshape(devices, HALF // devices, LANES))
    (copies,) = call(sum_shares, [shares.shape], shares)
    mine, beside = lax.optimization_barrier((to_all(copies).reshape(HALF, LANES), beside))
    return mine, swap_pairs(mine), beside


def on_device(acts, top_grad, kernel, ln_gain, ln_bias, w_in, b_in, w_out, layer_scale):
    sections = lax.axis_size("section")
    every = range(sections)
    is_last = (lax.axis_index("section") == sections - 1).astype(F32)
    odd = lax.rem(lax.axis_index("ty"), 2).astype(jnp.int32).reshape(1)
    field_shape, side, wide, hidden_shape = ((C, CELLS), (FOLD, LANES), (C, LANES), (HID, CELLS))
    edge_outs = [wide, MESSAGE, MESSAGE]
    acts_rows, top_rows = (acts.reshape(C * ROWS, LANES), top_grad.reshape(C * ROWS, LANES))

    field, to_right, to_left = call(take_field, [field_shape, side, side], acts_rows)
    left, right = to_sides(to_right, to_left, every)
    parameters = (
        top_rows, jnp.transpose(kernel, (1, 0, 2)), ln_gain, ln_bias, w_in[0], b_in, w_out[0].T, layer_scale,
    )
    cotan, taps, gain, shift_bias, scale, bias_in, weight_in, weight_out, w_in_gain, w_out_scale = call(
        prepare,
        [field_shape, (TAPS * C, LANES), (C, 1), (C, 1), (C, 1), (HID, 1), (C, HID), (C, HID), (C, HID), (HID, C)],
        *parameters, scratch=[p.shape for p in parameters] + [pltpu.SemaphoreType.DMA((len(parameters),))], copied=True,
    )
    strip, message_a, message_b = call(edges, edge_outs, field, left, right, odd)
    from_a, from_b = swap_rows(message_a, message_b, every)
    (own,) = call(functools.partial(conv_own, False), [field_shape], field, strip, taps, flops=CONV_FLOPS)
    around = (field, strip, from_a, from_b, odd)
    normed, inv, slope, hidden = call(
        forward,
        [field_shape, (1, CELLS), hidden_shape, hidden_shape],
        own, from_a, from_b, odd, taps, gain, shift_bias, weight_in, bias_in,
    )
    saved = (normed, inv, slope, w_in_gain, w_out_scale)

    cotan = cotan * is_last
    cotans, lefts, rights = [cotan], [], []
    strips = ()
    for section in reversed(every):
        only = (section,) if section else every
        if section == sections - 1:
            grad, to_right, to_left = call(first_step, [field_shape, side, side], cotan, *saved)
            grad_left, grad_right = to_sides(to_right, to_left, only)
            tile, grad = lax.optimization_barrier((saved[:3], grad))
            saved_right, saved_left = call(pack_saved, [SAVED_SIDE, SAVED_SIDE], *tile)
            grad_left, saved_right, saved_left = lax.optimization_barrier((grad_left, saved_right, saved_left))
            saved_sides = to_sides(saved_right, saved_left, range(sections - 1))
            first_strip, message_a, message_b = call(edges, edge_outs, grad, grad_left, grad_right, odd)
            grad_strip = first_strip
            strips = call(unpack_saved, [wide, (GROUP, LANES), (HID, LANES)], *saved_sides)
        elif section:
            grad, grad_strip, message_a, message_b = call(
                middle_step, [field_shape] + edge_outs, cotan, lefts[-1], rights[-1], odd, *saved, *strips
            )
        else:
            grad, grad_strip, message_a, message_b, cotan, grad_pre = call(
                functools.partial(last_step, len(cotans)), [field_shape] + edge_outs + [field_shape, hidden_shape],
                *cotans, *lefts, *rights, first_strip, odd, *saved, *strips,
            )
            payload = call(
                parameter_terms, [(HALF, LANES)] * 2,
                *around, grad, cotan, hidden, normed, grad_pre, gain, shift_bias, scale, weight_in, weight_out,
                scratch=[(PAYLOAD_ROWS, LANES)], flops=4 * CONV_FLOPS,
            )
        grad_a, grad_b = swap_rows(message_a, message_b, only)
        (own,) = call(
            functools.partial(conv_own, True), [field_shape], cotan, grad, grad_strip, taps, flops=CONV_FLOPS
        )
        if section:
            cotan, to_right, to_left = call(finish, [field_shape, side, side], own, grad_a, grad_b, odd, taps)
            cotan = lax.ppermute(cotan, "section", [(section, section - 1)])
            from_left, from_right = to_sides(to_right, to_left, only, 1)
            cotans.append(cotan)
            lefts.append(from_left)
            rights.append(from_right)
    *payload, own = sum_over_tiles(*payload, own)
    (input_grad,) = call(last_finish, [(C * ROWS, LANES)], own, grad_a, grad_b, odd, taps)
    grad_kernel, grad_gain, grad_bias, grad_w_in, grad_b_in, grad_w_out, grad_scale = call(
        parameter_grads,
        [(TAPS, 1, C), (1, C), (1, C), (C, HID), (1, HID), (C, HID), (1, C)],
        *payload, odd, scratch=[(PAYLOAD_ROWS, LANES)],
    )
    return (
        input_grad.reshape(1, 1, C, ROWS, LANES),
        jnp.transpose(grad_kernel, (1, 0, 2)),
        grad_gain,
        grad_bias,
        grad_w_in[None],
        grad_b_in,
        grad_w_out.T[None],
        grad_scale,
    )


def solution(mesh):
    placed = (
        P("section", None, None, "ty", "tx"),
        P(None, None, "ty", "tx"),
        P("section", None, None),
        P("section", None),
        P("section", None),
        P("section", None, None),
        P("section", None),
        P("section", None, None),
        P("section", None),
    )
    return jax.shard_map(
        on_device,
        mesh=mesh,
        in_specs=placed,
        out_specs=(
            P("section", None, None, "ty", "tx"),
            P("section", None, None),
            P("section", None),
            P("section", None),
            P("section", None, None),
            P("section", None),
            P("section", None, None),
            P("section", None),
        ),
        check_vma=False,
    )
```

```python
import functools

import jax
import jax.numpy as jnp
from jax import lax
from jax.experimental import pallas as pl
from jax.experimental.pallas import tpu as pltpu
from jax.sharding import PartitionSpec as P

KS = 7
TAPS = KS * KS
REACH = KS // 2
EPSILON = 1e-06
LANES = 128
GROUP = 8
ROWS = 8
C = 96
HID = 384
CELLS = ROWS * LANES
FOLD = 24
CHUNK = 256
PAYLOAD_ROWS = 1024
F32 = jnp.float32
BF16 = jnp.bfloat16
CONV_FLOPS = 2 * TAPS * C * CELLS
TILES = ("ty", "tx")


def call(kernel, outs, *operands, scratch=(), flops=0, copied=False):
    whole = pl.BlockSpec(memory_space=pltpu.VMEM)
    specs = [
        pl.BlockSpec(memory_space=pltpu.SMEM if operand.dtype == jnp.int32 else pltpu.HBM if copied else pltpu.VMEM)
        for operand in operands
    ]
    spaces = [pltpu.VMEM(shape, F32) if isinstance(shape, tuple) else shape for shape in scratch]
    return pl.pallas_call(
        kernel,
        out_shape=[jax.ShapeDtypeStruct(shape, F32) for shape in outs],
        in_specs=specs,
        out_specs=[whole] * len(outs),
        scratch_shapes=spaces,
        compiler_params=pltpu.CompilerParams(vmem_limit_bytes=28 * 1024 * 1024),
        cost_estimate=pl.CostEstimate(flops=flops, bytes_accessed=0, transcendentals=0) if flops else None,
    )(*operands)


def roll(value, shift):
    return pltpu.roll(value, shift % LANES, 1)


def lane_of(rows):
    return lax.broadcasted_iota(jnp.int32, (rows, LANES), 1)


def block(row):
    return pl.ds(row * LANES, LANES)


def split(value):
    high = value.astype(BF16)
    low = (value - high.astype(F32)).astype(BF16)
    return high, low


def product(left, right, dims):
    def part(one, two):
        return lax.dot_general(one, two, (dims, ((), ())), preferred_element_type=F32)

    return part(left[0], right[0]) + (part(left[0], right[1]) + part(left[1], right[0]))


ROW_COL = ((1,), (0,))
COL_COL = ((0,), (0,))
ROW_ROW = ((1,), (1,))


ACTS_REACH = 2 * REACH
ACTS_SIDE = 64
SIDE = 32


def pack_edges(field_ref, right_ref, left_ref, width=REACH, side=SIDE):
    rows = out_rows = C * side // LANES
    lane = lane_of(out_rows)
    for edge, out_ref in ((LANES - width, right_ref), (0, left_ref)):
        folded = jnp.zeros((out_rows, LANES), F32)
        for part in range(LANES // side):
            for row in range(ROWS):
                at = side * part + width * row
                moved = roll(field_ref[pl.ds(part * rows, rows), block(row)], at - edge)
                folded = jnp.where((lane >= at) & (lane < at + width), moved, folded)
        out_ref[...] = folded


def unfold(left, right, side=SIDE):
    lane = lane_of(left.shape[0])
    parts = []
    for part in range(LANES // side):
        theirs = roll(left, -side * part)
        parts.append(jnp.where(lane < side, theirs, jnp.where(lane < 2 * side, roll(right, side - side * part), 0.0)))
    return jnp.concatenate(parts, axis=0)


def shifted_row(row, left, right, lane, distance):
    if distance > 0:
        return roll(jnp.where(lane < distance, right, row), -distance)
    if distance < 0:
        return roll(jnp.where(lane >= LANES + distance, left, row), -distance)
    return row


NEAR = (REACH, 0, SIDE)
WIDE = (ACTS_REACH, REACH, ACTS_SIDE)


def with_edges(value, strip, row, layout):
    width, skipped, side = layout
    return value, roll(strip, LANES - REACH - skipped - width * row), roll(strip, -side - width * row)


def tap_of(taps_ref, tap, group):
    return taps_ref[pl.ds(tap * C + group, GROUP), :]


def take_field(acts_ref, field_ref, right_ref, left_ref):
    for row in range(ROWS):
        field_ref[:, block(row)] = acts_ref[pl.ds(row, C, stride=ROWS), :]
    pack_edges(field_ref, right_ref, left_ref, ACTS_REACH, ACTS_SIDE)


def column(row):
    return jnp.broadcast_to(row, (GROUP, row.shape[1])).T[:, :1]


def prepare(*refs):
    count = 8
    sources, outs, held = refs[: count], refs[count : -count - 1], refs[-count - 1 : -1]
    sems = refs[-1]
    copies = [pltpu.make_async_copy(source, target, sems.at[i]) for i, (source, target) in enumerate(zip(sources, held))]
    for copy in copies:
        copy.start()
    for copy in copies:
        copy.wait()
    top_ref, kernel_ref, gain_row, bias_row, w_in_ref, b_in_row, w_out_ref, scale_row = held
    cotan_ref, right_ref, left_ref, taps_ref, gain_ref, bias_ref, scale_ref, b_in_ref = outs[:8]
    w_in_out, w_out_out, w_in_gain_ref, w_out_scale_ref = outs[8:]
    for row in range(ROWS):
        cotan_ref[:, block(row)] = top_ref[pl.ds(row, C, stride=ROWS), :]
    pack_edges(cotan_ref, right_ref, left_ref)
    taps = kernel_ref[:, 0, :].T
    for tap in range(TAPS):
        taps_ref[pl.ds(tap * C, C), :] = jnp.broadcast_to(taps[:, tap : tap + 1], (C, LANES))
    gain_ref[...] = column(gain_row[...])
    bias_ref[...] = column(bias_row[...])
    scale_ref[...] = column(scale_row[...])
    b_in_ref[...] = column(b_in_row[...])
    w_in_out[...] = w_in_ref[...]
    w_out_out[...] = w_out_ref[...]
    w_in_gain_ref[...] = w_in_ref[...] * gain_ref[...]
    w_out_scale_ref[...] = (w_out_ref[...] * scale_ref[...]).T


STRIP_AT = REACH * C
MESSAGE = (STRIP_AT + C, LANES)


def write_messages(field_ref, strip_ref, odd_ref, a_ref, b_ref):
    odd = odd_ref[0]
    for first, out_ref in (((1 - odd) * (ROWS - REACH), a_ref), (odd * (ROWS - REACH), b_ref)):
        for index in range(REACH):
            lanes = pl.ds(pl.multiple_of((first + index) * LANES, LANES), LANES)
            out_ref[pl.ds(index * C, C), :] = field_ref[:, lanes]
        out_ref[pl.ds(STRIP_AT, C), :] = strip_ref[...]


def outer_pieces(group, a_ref, b_ref, odd):
    rows = {}
    for index in range(REACH + 1):
        at = pl.ds(index * C + group, GROUP)
        from_a, from_b = a_ref[at, :], b_ref[at, :]
        rows[index] = (jnp.where(odd, from_a, from_b), jnp.where(odd, from_b, from_a))
    above, below = rows.pop(REACH)
    found = {}
    for index in range(REACH):
        found[index - REACH] = (rows[index][0], above, ROWS - REACH + index)
        found[ROWS + index] = (rows[index][1], below, index)
    return found


def outer_rows(group, a_ref, b_ref, odd, layout):
    return {at: with_edges(*piece, layout) for at, piece in outer_pieces(group, a_ref, b_ref, odd).items()}


def own_pieces(channels, field_ref, strip_ref):
    strip = strip_ref[channels, :]
    return {row: (field_ref[channels, block(row)], strip, row) for row in range(ROWS)}


def own_rows(channels, field_ref, strip_ref, layout):
    return {at: with_edges(*piece, layout) for at, piece in own_pieces(channels, field_ref, strip_ref).items()}


def edges(field_ref, left_ref, right_ref, odd_ref, strip_ref, a_ref, b_ref):
    strip_ref[...] = unfold(left_ref[...], right_ref[...], ACTS_SIDE)
    write_messages(field_ref, strip_ref, odd_ref, a_ref, b_ref)


def tap_index(a, b, flipped):
    tap = a * KS + b
    return TAPS - 1 - tap if flipped else tap


def conv_own(flipped, *refs):
    start_ref = refs[0] if flipped else None
    field_ref, strip_ref, taps_ref, out_ref = refs[-4:]
    lane = lane_of(GROUP)

    def conv_group(index, carry):
        group = pl.multiple_of(index * GROUP, GROUP)
        channels = pl.ds(group, GROUP)
        rows = own_rows(channels, field_ref, strip_ref, NEAR if flipped else WIDE)
        if flipped:
            sums = [start_ref[channels, block(row)] for row in range(ROWS)]
        else:
            sums = [jnp.zeros((GROUP, LANES), F32)] * ROWS
        for b in range(KS):
            moved = [shifted_row(*rows[row], lane, b - REACH) for row in range(ROWS)]
            for a in range(KS):
                weight = tap_of(taps_ref, tap_index(a, b, flipped), group)
                for row in range(ROWS):
                    if 0 <= row + a - REACH < ROWS:
                        sums[row] = sums[row] + weight * moved[row + a - REACH]
        for row in range(ROWS):
            out_ref[channels, block(row)] = sums[row]
        return carry

    lax.fori_loop(0, C // GROUP, conv_group, 0)


def conv_edges(flipped, own_ref, a_ref, b_ref, odd_ref, taps_ref, put):
    odd = odd_ref[0] == 1
    lane = lane_of(GROUP)

    def conv_group(index, carry):
        group = pl.multiple_of(index * GROUP, GROUP)
        channels = pl.ds(group, GROUP)
        rows = outer_rows(group, a_ref, b_ref, odd, NEAR if flipped else WIDE)
        sums = [own_ref[channels, block(row)] for row in range(ROWS)]
        for b in range(KS):
            moved = {at: shifted_row(*row, lane, b - REACH) for at, row in rows.items()}
            for a in range(KS):
                if a == REACH:
                    continue
                weight = tap_of(taps_ref, tap_index(a, b, flipped), group)
                for row in range(ROWS):
                    if row + a - REACH in moved:
                        sums[row] = sums[row] + weight * moved[row + a - REACH]
        put(group, sums)
        return carry

    lax.fori_loop(0, C // GROUP, conv_group, 0)


SPAN = 3 * REACH


def side_sums(side, pieces, taps_ref, group, lane):
    packed = jnp.zeros((GROUP, LANES), F32)
    for place, at in enumerate(sorted(pieces)):
        row, strip, index = pieces[at]
        start = SPAN * place
        if side == 0:
            parts = ((strip, ACTS_REACH * index, start, ACTS_REACH), (row, 0, start + ACTS_REACH, REACH))
        else:
            parts = ((row, LANES - REACH, start, REACH), (strip, ACTS_SIDE + ACTS_REACH * index, start + REACH, ACTS_REACH))
        for value, origin, to, width in parts:
            packed = jnp.where((lane >= to) & (lane < to + width), roll(value, to - origin), packed)
    total = jnp.zeros((GROUP, LANES), F32)
    for tap in range(TAPS):
        total = total + tap_of(taps_ref, tap, group) * roll(packed, -(SPAN * (tap // KS) + tap % KS))
    result = jnp.zeros((GROUP, LANES), F32)
    for row in range(ROWS):
        to = SIDE * side + REACH * row
        result = jnp.where((lane >= to) & (lane < to + REACH), roll(total, to - SPAN * row), result)
    return result


def forward(
    field_ref, strip_ref, own_ref, a_ref, b_ref, odd_ref, taps_ref, gain_ref, bias_ref, w_in_ref, b_in_ref,
    normed_ref, inv_ref, slope_ref, hidden_ref, side_normed_ref, side_inv_ref, side_slope_ref,
):
    def put(group, sums):
        for row in range(ROWS):
            normed_ref[pl.ds(group, GROUP), block(row)] = sums[row]

    conv_edges(False, own_ref, a_ref, b_ref, odd_ref, taps_ref, put)
    odd = odd_ref[0] == 1
    lane = lane_of(GROUP)

    def side_group(index, carry):
        group = pl.multiple_of(index * GROUP, GROUP)
        channels = pl.ds(group, GROUP)
        pieces = outer_pieces(group, a_ref, b_ref, odd) | own_pieces(channels, field_ref, strip_ref)
        left, right = (side_sums(side, pieces, taps_ref, group, lane) for side in range(2))
        side_normed_ref[channels, :] = left + right
        return carry

    lax.fori_loop(0, C // GROUP, side_group, 0)
    w_in = split(w_in_ref[...])

    def finish_cells(conv_out):
        centred = conv_out - jnp.mean(conv_out, axis=0, keepdims=True)
        inv = lax.rsqrt(jnp.mean(centred * centred, axis=0, keepdims=True) + EPSILON)
        normed = centred * inv
        lifted = normed * gain_ref[...] + bias_ref[...]
        pre_act = product(w_in, split(lifted), COL_COL) + b_in_ref[...]
        gate = 0.5 * (1.0 + lax.erf(pre_act * 0.7071067811865476))
        slope = gate + pre_act * jnp.exp(-0.5 * pre_act * pre_act) * 0.3989422804014327
        return normed, inv, slope, pre_act * gate

    for start in range(0, CELLS, CHUNK):
        cells = pl.ds(start, CHUNK)
        normed_ref[:, cells], inv_ref[:, cells], slope_ref[:, cells], hidden_ref[:, cells] = finish_cells(normed_ref[:, cells])
    side_normed_ref[...], side_inv_ref[...], side_slope_ref[...], unused = finish_cells(side_normed_ref[...])


def grad_at(cotan, w_out, w_in, normed, inv, slope):
    grad_pre = product(w_out, split(cotan), ROW_COL) * slope
    grad_normed = product(w_in, split(grad_pre), ROW_COL)
    mean = jnp.mean(grad_normed, axis=0, keepdims=True)
    along = jnp.mean(grad_normed * normed, axis=0, keepdims=True)
    return grad_pre, inv * (grad_normed - mean - normed * along)


def step_tile(cotan_refs, saved, grad_ref, keep):
    normed_ref, inv_ref, slope_ref, w_in_gain_ref, w_out_scale_ref = saved
    w_out = split(w_out_scale_ref[...])
    w_in = split(w_in_gain_ref[...])
    for start in range(0, CELLS, CHUNK):
        cells = pl.ds(start, CHUNK)
        cotan = sum(ref[:, cells] for ref in cotan_refs)
        grad_pre, grad = grad_at(cotan, w_out, w_in, normed_ref[:, cells], inv_ref[:, cells], slope_ref[:, cells])
        keep(cells, cotan, grad_pre)
        grad_ref[:, cells] = grad
    return w_out, w_in


def ignore(cells, cotan, grad_pre):
    pass


def step_sides(lefts, rights, weights, strips):
    left, right = sum(ref[...] for ref in lefts), sum(ref[...] for ref in rights)
    normed_ref, inv_ref, slope_ref = strips
    cotan = unfold(left, right)
    return grad_at(cotan, *weights, normed_ref[...], inv_ref[...], slope_ref[...])[1]


def middle_step(cotan_ref, from_left, from_right, odd_ref, *refs):
    saved, strips, (grad_ref, strip_ref, a_ref, b_ref) = refs[:5], refs[5:8], refs[8:]
    weights = step_tile((cotan_ref,), saved, grad_ref, ignore)
    strip_ref[...] = step_sides((from_left,), (from_right,), weights, strips)
    write_messages(grad_ref, strip_ref, odd_ref, a_ref, b_ref)


def last_step(count, *refs):
    cotans, lefts, rights, odd_ref = refs[:count], refs[count : 2 * count], refs[2 * count : 3 * count], refs[3 * count]
    refs = refs[3 * count + 1 :]
    saved, strips = refs[:5], refs[5:8]
    grad_ref, strip_ref, a_ref, b_ref, cotan_ref, grad_pre_ref = refs[8:]

    def keep(cells, cotan, grad_pre):
        cotan_ref[:, cells] = cotan
        grad_pre_ref[:, cells] = grad_pre

    weights = step_tile(cotans, saved, grad_ref, keep)
    strip_ref[...] = step_sides(lefts, rights, weights, strips)
    write_messages(grad_ref, strip_ref, odd_ref, a_ref, b_ref)


def finish(own_ref, a_ref, b_ref, odd_ref, taps_ref, out_ref, right_ref, left_ref):
    def put(group, sums):
        for row in range(ROWS):
            out_ref[pl.ds(group, GROUP), block(row)] = sums[row]

    conv_edges(True, own_ref, a_ref, b_ref, odd_ref, taps_ref, put)
    pack_edges(out_ref, right_ref, left_ref)


def last_finish(own_ref, a_ref, b_ref, odd_ref, taps_ref, out_ref):
    def put(group, sums):
        for row in range(ROWS):
            out_ref[pl.ds(group * ROWS + row, GROUP, stride=ROWS), :] = sums[row]

    conv_edges(True, own_ref, a_ref, b_ref, odd_ref, taps_ref, put)


LIFT_ROWS = C + GROUP
OUT_AT = 0
IN_AT = OUT_AT + C * HID // LANES
TAPS_AT = IN_AT + LIFT_ROWS * HID // LANES
USED_ROWS = TAPS_AT + C


HALF = PAYLOAD_ROWS // 2


def half_of(odd):
    return pl.ds(pl.multiple_of(odd * HALF, HALF), HALF)


def parameter_terms(
    field_ref, strip_ref, a_ref, b_ref, odd_ref, grad_ref, cotan_ref, hidden_ref, normed_ref, grad_pre_ref,
    gain_ref, bias_ref, scale_ref, w_in_ref, w_out_ref,
    mine_ref, theirs_ref, payload_ref,
):
    odd = odd_ref[0] == 1
    lane = lane_of(GROUP)

    def taps_group(index, carry):
        group = pl.multiple_of(index * GROUP, GROUP)
        found = outer_rows(group, a_ref, b_ref, odd, WIDE) | own_rows(pl.ds(group, GROUP), field_ref, strip_ref, WIDE)
        rows = [found[row] for row in sorted(found)]
        grads = [grad_ref[pl.ds(group, GROUP), block(row)] for row in range(ROWS)]
        result = jnp.zeros((GROUP, LANES), F32)
        for b in range(KS):
            moved = [shifted_row(*row, lane, b - REACH) for row in rows]
            for a in range(KS):
                terms = [grads[row] * moved[row + a] for row in range(ROWS)]
                while len(terms) > 1:
                    terms = [one + two for one, two in zip(terms[0::2], terms[1::2])]
                total = jnp.sum(terms[0], axis=1, keepdims=True)
                result = jnp.where(lane == a * KS + b, total, result)
        payload_ref[pl.ds(TAPS_AT + group, GROUP), :] = result
        return carry

    lax.fori_loop(0, C // GROUP, taps_group, 0)
    grad_w_out = product(split(cotan_ref[...]), split(hidden_ref[...]), ROW_ROW)
    ones = jnp.where(lax.broadcasted_iota(jnp.int32, (GROUP, CELLS), 0) == 0, 1.0, 0.0)
    lifted = jnp.concatenate([normed_ref[...], ones], axis=0)
    grad_w_in = product(split(lifted), split(grad_pre_ref[...]), ROW_ROW)
    grad_b_in = grad_w_in[C : C + 1, :]
    columns = (w_in_ref[...] * grad_w_in[:C, :], w_in_ref[...] * grad_b_in, w_out_ref[...] * grad_w_out)
    lane = lane_of(C)
    for index, terms in enumerate(columns):
        total = jnp.sum(terms, axis=1, keepdims=True)
        taps = payload_ref[pl.ds(TAPS_AT, C), :]
        payload_ref[pl.ds(TAPS_AT, C), :] = jnp.where(lane == TAPS + index, total, taps)
    grad_w_out = grad_w_out * scale_ref[...]
    grad_weights = grad_w_in[:C, :] * gain_ref[...] + bias_ref[...] * grad_b_in
    for part in range(HID // LANES):
        lanes = slice(part * LANES, (part + 1) * LANES)
        at = IN_AT + part * LIFT_ROWS
        payload_ref[pl.ds(OUT_AT + part * C, C), :] = grad_w_out[:, lanes]
        payload_ref[pl.ds(at, C), :] = grad_weights[:, lanes]
        payload_ref[pl.ds(at + C, GROUP), :] = grad_w_in[C:, lanes]
    payload_ref[pl.ds(USED_ROWS, PAYLOAD_ROWS - USED_ROWS), :] = jnp.zeros((PAYLOAD_ROWS - USED_ROWS, LANES), F32)
    mine_ref[...] = payload_ref[half_of(odd_ref[0]), :]
    theirs_ref[...] = payload_ref[half_of(1 - odd_ref[0]), :]


def add_halves(mine_ref, theirs_ref, a_ref, b_ref, out_ref):
    out_ref[...] = mine_ref[...] + theirs_ref[...]


def sum_shares(shares_ref, out_ref):
    devices = out_ref.shape[0]
    terms = [shares_ref[device] for device in range(devices)]
    while len(terms) > 1:
        terms = [one + two for one, two in zip(terms[0::2], terms[1::2])]
    for device in range(devices):
        out_ref[device] = terms[0]


def parameter_grads(
    mine_ref, theirs_ref, odd_ref,
    kernel_out, gain_out, bias_out, w_in_out, b_in_out, w_out_out, scale_out,
    payload_ref,
):
    payload_ref[half_of(odd_ref[0]), :] = mine_ref[...]
    payload_ref[half_of(1 - odd_ref[0]), :] = theirs_ref[...]
    by_tap = payload_ref[pl.ds(TAPS_AT, C), :].T
    kernel_out[:, 0, :] = by_tap[:TAPS, :]
    for index, out_ref in enumerate((gain_out, bias_out, scale_out)):
        out_ref[...] = by_tap[TAPS + index : TAPS + index + 1, :]
    for part in range(HID // LANES):
        hidden = pl.ds(part * LANES, LANES)
        at = IN_AT + part * LIFT_ROWS
        w_out_out[:, hidden] = payload_ref[pl.ds(OUT_AT + part * C, C), :]
        w_in_out[:, hidden] = payload_ref[pl.ds(at, C), :]
        b_in_out[:, hidden] = payload_ref[pl.ds(at + C, 1), :]


def pairs(axis, sections, odd_pairs):
    size = lax.axis_size(axis)
    routes = []
    for section in sections:
        for tile in range(1 if odd_pairs else 0, size - 1, 2):
            here = section * size + tile
            routes += [(here, here + 1), (here + 1, here)]
    return routes


def swap_rows(message_a, message_b, sections):
    axes = ("section", "ty")
    return (
        lax.ppermute(message_a, axes, pairs("ty", sections, False)),
        lax.ppermute(message_b, axes, pairs("ty", sections, True)),
    )


def to_sides(to_right, to_left, sections, back=0):
    size = lax.axis_size("tx")
    right = [(s * size + i, (s - back) * size + i + 1) for s in sections for i in range(size - 1)]
    left = [(s * size + i + 1, (s - back) * size + i) for s in sections for i in range(size - 1)]
    axes = ("section", "tx")
    return lax.ppermute(to_right, axes, right), lax.ppermute(to_left, axes, left)


def swap_pairs(half):
    return lax.ppermute(half, "ty", [(tile, tile ^ 1) for tile in range(lax.axis_size("ty"))])


def sum_over_tiles(mine, theirs, rows):
    columns = lax.axis_size("tx")
    tiles = lax.axis_size("ty")
    groups = [[tile * columns + i for tile in range(odd, tiles, 2) for i in range(columns)] for odd in range(2)]
    devices = len(groups[0])

    def to_all(shares):
        return lax.all_to_all(shares, TILES, 0, 0, axis_index_groups=groups)

    (half,) = call(add_halves, [(HALF, LANES)], mine, swap_pairs(theirs), *rows)
    shares = to_all(half.reshape(devices, HALF // devices, LANES))
    (copies,) = call(sum_shares, [shares.shape], shares)
    mine = to_all(copies).reshape(HALF, LANES)
    return mine, swap_pairs(mine)


def on_device(acts, top_grad, kernel, ln_gain, ln_bias, w_in, b_in, w_out, layer_scale):
    sections = lax.axis_size("section")
    every = range(sections)
    is_last = (lax.axis_index("section") == sections - 1).astype(F32)
    odd = lax.rem(lax.axis_index("ty"), 2).astype(jnp.int32).reshape(1)
    field_shape, side, wide, hidden_shape = ((C, CELLS), (FOLD, LANES), (C, LANES), (HID, CELLS))
    edge_outs = [wide, MESSAGE, MESSAGE]
    acts_rows, top_rows = (acts.reshape(C * ROWS, LANES), top_grad.reshape(C * ROWS, LANES))

    acts_side = (C * ACTS_SIDE // LANES, LANES)
    field, to_right, to_left = call(take_field, [field_shape, acts_side, acts_side], acts_rows)
    left, right = to_sides(to_right, to_left, every)
    parameters = (
        top_rows, jnp.transpose(kernel, (1, 0, 2)), ln_gain, ln_bias, w_in[0], b_in, w_out[0].T, layer_scale,
    )
    cotan, top_right, top_left, taps, gain, shift_bias, scale, bias_in, weight_in, weight_out, w_in_gain, w_out_scale = call(
        prepare,
        [field_shape, side, side, (TAPS * C, LANES), (C, 1), (C, 1), (C, 1), (HID, 1), (C, HID), (C, HID), (C, HID), (HID, C)],
        *parameters, scratch=[p.shape for p in parameters] + [pltpu.SemaphoreType.DMA((len(parameters),))], copied=True,
    )
    top_left, top_right = to_sides(top_right, top_left, (sections - 1,))
    strip, message_a, message_b = call(edges, edge_outs, field, left, right, odd)
    from_a, from_b = swap_rows(message_a, message_b, every)
    (own,) = call(functools.partial(conv_own, False), [field_shape], field, strip, taps, flops=CONV_FLOPS)
    around = (field, strip, from_a, from_b, odd)
    normed, inv, slope, hidden, *strips = call(
        forward,
        [field_shape, (1, CELLS), hidden_shape, hidden_shape, wide, (1, LANES), (HID, LANES)],
        field, strip, own, from_a, from_b, odd, taps, gain, shift_bias, weight_in, bias_in,
    )
    saved = (normed, inv, slope, w_in_gain, w_out_scale)

    cotan = cotan * is_last
    cotans, lefts, rights = [cotan], [top_left], [top_right]
    for section in reversed(every):
        only = (section,) if section else every
        if section:
            grad, grad_strip, message_a, message_b = call(
                middle_step, [field_shape] + edge_outs, cotan, lefts[-1], rights[-1], odd, *saved, *strips
            )
        else:
            grad, grad_strip, message_a, message_b, cotan, grad_pre = call(
                functools.partial(last_step, len(cotans)), [field_shape] + edge_outs + [field_shape, hidden_shape],
                *cotans, *lefts, *rights, odd, *saved, *strips,
            )
            payload = call(
                parameter_terms, [(HALF, LANES)] * 2,
                *around, grad, cotan, hidden, normed, grad_pre, gain, shift_bias, scale, weight_in, weight_out,
                scratch=[(PAYLOAD_ROWS, LANES)], flops=4 * CONV_FLOPS,
            )
        grad_a, grad_b = swap_rows(message_a, message_b, only)
        (own,) = call(
            functools.partial(conv_own, True), [field_shape], cotan, grad, grad_strip, taps, flops=CONV_FLOPS
        )
        if section:
            cotan, to_right, to_left = call(finish, [field_shape, side, side], own, grad_a, grad_b, odd, taps)
            from_left, from_right = to_sides(to_right, to_left, only, 1)
            cotan = lax.ppermute(cotan, "section", [(section, section - 1)])
            cotans.append(cotan)
            lefts.append(from_left)
            rights.append(from_right)
    payload = sum_over_tiles(*payload, (grad_a, grad_b))
    (input_grad,) = call(last_finish, [(C * ROWS, LANES)], own, grad_a, grad_b, odd, taps)
    grad_kernel, grad_gain, grad_bias, grad_w_in, grad_b_in, grad_w_out, grad_scale = call(
        parameter_grads,
        [(TAPS, 1, C), (1, C), (1, C), (C, HID), (1, HID), (C, HID), (1, C)],
        *payload, odd, scratch=[(PAYLOAD_ROWS, LANES)],
    )
    return (
        input_grad.reshape(1, 1, C, ROWS, LANES),
        jnp.transpose(grad_kernel, (1, 0, 2)),
        grad_gain,
        grad_bias,
        grad_w_in[None],
        grad_b_in,
        grad_w_out.T[None],
        grad_scale,
    )


def solution(mesh):
    placed = (
        P("section", None, None, "ty", "tx"),
        P(None, None, "ty", "tx"),
        P("section", None, None),
        P("section", None),
        P("section", None),
        P("section", None, None),
        P("section", None),
        P("section", None, None),
        P("section", None),
    )
    return jax.shard_map(
        on_device,
        mesh=mesh,
        in_specs=placed,
        out_specs=(
            P("section", None, None, "ty", "tx"),
            P("section", None, None),
            P("section", None),
            P("section", None),
            P("section", None, None),
            P("section", None),
            P("section", None, None),
            P("section", None),
        ),
        check_vma=False,
    )
```

```python
import functools

import jax
import jax.numpy as jnp
from jax import lax
from jax.experimental import pallas as pl
from jax.experimental.pallas import tpu as pltpu
from jax.sharding import PartitionSpec as P

KS = 7
TAPS = KS * KS
REACH = KS // 2
EPSILON = 1e-06
LANES = 128
GROUP = 8
ROWS = 8
C = 96
HID = 384
CELLS = ROWS * LANES
FOLD = 24
CHUNK = 256
PAYLOAD_ROWS = 1024
F32 = jnp.float32
BF16 = jnp.bfloat16
CONV_FLOPS = 2 * TAPS * C * CELLS
TILES = ("ty", "tx")


def call(kernel, outs, *operands, scratch=(), flops=0, copied=False):
    whole = pl.BlockSpec(memory_space=pltpu.VMEM)
    specs = [
        pl.BlockSpec(memory_space=pltpu.SMEM if operand.dtype == jnp.int32 else pltpu.HBM if copied else pltpu.VMEM)
        for operand in operands
    ]
    spaces = [pltpu.VMEM(shape, F32) if isinstance(shape, tuple) else shape for shape in scratch]
    return pl.pallas_call(
        kernel,
        out_shape=[jax.ShapeDtypeStruct(shape, F32) for shape in outs],
        in_specs=specs,
        out_specs=[whole] * len(outs),
        scratch_shapes=spaces,
        compiler_params=pltpu.CompilerParams(vmem_limit_bytes=28 * 1024 * 1024),
        cost_estimate=pl.CostEstimate(flops=flops, bytes_accessed=0, transcendentals=0) if flops else None,
    )(*operands)


def roll(value, shift):
    return pltpu.roll(value, shift % LANES, 1)


def lane_of(rows):
    return lax.broadcasted_iota(jnp.int32, (rows, LANES), 1)


def block(row):
    return pl.ds(row * LANES, LANES)


def split(value):
    high = value.astype(BF16)
    low = (value - high.astype(F32)).astype(BF16)
    return high, low


def product(left, right, dims):
    def part(one, two):
        return lax.dot_general(one, two, (dims, ((), ())), preferred_element_type=F32)

    return part(left[0], right[0]) + (part(left[0], right[1]) + part(left[1], right[0]))


ROW_COL = ((1,), (0,))
COL_COL = ((0,), (0,))
ROW_ROW = ((1,), (1,))


ACTS_REACH = 2 * REACH
ACTS_SIDE = 64
SIDE = 32


def pack_edges(field_ref, right_ref, left_ref, width=REACH, side=SIDE):
    rows = out_rows = C * side // LANES
    lane = lane_of(out_rows)
    for edge, out_ref in ((LANES - width, right_ref), (0, left_ref)):
        folded = jnp.zeros((out_rows, LANES), F32)
        for part in range(LANES // side):
            for row in range(ROWS):
                at = side * part + width * row
                moved = roll(field_ref[pl.ds(part * rows, rows), block(row)], at - edge)
                folded = jnp.where((lane >= at) & (lane < at + width), moved, folded)
        out_ref[...] = folded


def unfold(left, right, side=SIDE):
    lane = lane_of(left.shape[0])
    parts = []
    for part in range(LANES // side):
        theirs = roll(left, -side * part)
        parts.append(jnp.where(lane < side, theirs, jnp.where(lane < 2 * side, roll(right, side - side * part), 0.0)))
    return jnp.concatenate(parts, axis=0)


def shifted_row(row, left, right, lane, distance):
    if distance > 0:
        return roll(jnp.where(lane < distance, right, row), -distance)
    if distance < 0:
        return roll(jnp.where(lane >= LANES + distance, left, row), -distance)
    return row


NEAR = (REACH, 0, SIDE)
WIDE = (ACTS_REACH, REACH, ACTS_SIDE)


def with_edges(value, strip, row, layout):
    width, skipped, side = layout
    return value, roll(strip, LANES - REACH - skipped - width * row), roll(strip, -side - width * row)


def tap_of(taps_ref, tap, group):
    return taps_ref[pl.ds(tap * C + group, GROUP), :]


ACTS_ROWS = C * ACTS_SIDE // LANES
SIDE_MESSAGE = (ACTS_ROWS + FOLD, LANES)


def take_fields(acts_ref, top_ref, field_ref, cotan_ref, right_ref, left_ref):
    for row in range(ROWS):
        field_ref[:, block(row)] = acts_ref[pl.ds(row, C, stride=ROWS), :]
        cotan_ref[:, block(row)] = top_ref[pl.ds(row, C, stride=ROWS), :]
    wide, near = pl.ds(0, ACTS_ROWS), pl.ds(ACTS_ROWS, FOLD)
    pack_edges(field_ref, right_ref.at[wide, :], left_ref.at[wide, :], ACTS_REACH, ACTS_SIDE)
    pack_edges(cotan_ref, right_ref.at[near, :], left_ref.at[near, :])


def column(row):
    return jnp.broadcast_to(row, (GROUP, row.shape[1])).T[:, :1]


def prepare(*refs):
    count = 7
    sources, outs, held = refs[: count], refs[count : -count - 1], refs[-count - 1 : -1]
    sems = refs[-1]
    copies = [pltpu.make_async_copy(source, target, sems.at[i]) for i, (source, target) in enumerate(zip(sources, held))]
    for copy in copies:
        copy.start()
    for copy in copies:
        copy.wait()
    kernel_ref, gain_row, bias_row, w_in_ref, b_in_row, w_out_ref, scale_row = held
    taps_ref, gain_ref, bias_ref, scale_ref, b_in_ref, w_in_out, w_out_out, w_in_gain_ref, w_out_scale_ref = outs
    taps = kernel_ref[:, 0, :].T
    for tap in range(TAPS):
        taps_ref[pl.ds(tap * C, C), :] = jnp.broadcast_to(taps[:, tap : tap + 1], (C, LANES))
    gain_ref[...] = column(gain_row[...])
    bias_ref[...] = column(bias_row[...])
    scale_ref[...] = column(scale_row[...])
    b_in_ref[...] = column(b_in_row[...])
    w_in_out[...] = w_in_ref[...]
    w_out_out[...] = w_out_ref[...]
    w_in_gain_ref[...] = w_in_ref[...] * gain_ref[...]
    w_out_scale_ref[...] = (w_out_ref[...] * scale_ref[...]).T


STRIP_AT = REACH * C
MESSAGE = (STRIP_AT + C, LANES)


def write_messages(field_ref, strip_ref, odd_ref, a_ref, b_ref):
    odd = odd_ref[0]
    for first, out_ref in (((1 - odd) * (ROWS - REACH), a_ref), (odd * (ROWS - REACH), b_ref)):
        for index in range(REACH):
            lanes = pl.ds(pl.multiple_of((first + index) * LANES, LANES), LANES)
            out_ref[pl.ds(index * C, C), :] = field_ref[:, lanes]
        out_ref[pl.ds(STRIP_AT, C), :] = strip_ref[...]


def outer_pieces(group, a_ref, b_ref, odd):
    rows = {}
    for index in range(REACH + 1):
        at = pl.ds(index * C + group, GROUP)
        from_a, from_b = a_ref[at, :], b_ref[at, :]
        rows[index] = (jnp.where(odd, from_a, from_b), jnp.where(odd, from_b, from_a))
    above, below = rows.pop(REACH)
    found = {}
    for index in range(REACH):
        found[index - REACH] = (rows[index][0], above, ROWS - REACH + index)
        found[ROWS + index] = (rows[index][1], below, index)
    return found


def outer_rows(group, a_ref, b_ref, odd, layout):
    return {at: with_edges(*piece, layout) for at, piece in outer_pieces(group, a_ref, b_ref, odd).items()}


def own_pieces(channels, field_ref, strip_ref):
    strip = strip_ref[channels, :]
    return {row: (field_ref[channels, block(row)], strip, row) for row in range(ROWS)}


def own_rows(channels, field_ref, strip_ref, layout):
    return {at: with_edges(*piece, layout) for at, piece in own_pieces(channels, field_ref, strip_ref).items()}


def edges(field_ref, left_ref, right_ref, odd_ref, strip_ref, a_ref, b_ref):
    wide = pl.ds(0, ACTS_ROWS)
    strip_ref[...] = unfold(left_ref[wide, :], right_ref[wide, :], ACTS_SIDE)
    write_messages(field_ref, strip_ref, odd_ref, a_ref, b_ref)


def tap_index(a, b, flipped):
    tap = a * KS + b
    return TAPS - 1 - tap if flipped else tap


def conv_own(flipped, *refs):
    start_ref = refs[0] if flipped else None
    field_ref, strip_ref, taps_ref, out_ref = refs[-4:]
    lane = lane_of(GROUP)

    def conv_group(index, carry):
        group = pl.multiple_of(index * GROUP, GROUP)
        channels = pl.ds(group, GROUP)
        rows = own_rows(channels, field_ref, strip_ref, NEAR if flipped else WIDE)
        if flipped:
            sums = [start_ref[channels, block(row)] for row in range(ROWS)]
        else:
            sums = [jnp.zeros((GROUP, LANES), F32)] * ROWS
        for b in range(KS):
            moved = [shifted_row(*rows[row], lane, b - REACH) for row in range(ROWS)]
            for a in range(KS):
                weight = tap_of(taps_ref, tap_index(a, b, flipped), group)
                for row in range(ROWS):
                    if 0 <= row + a - REACH < ROWS:
                        sums[row] = sums[row] + weight * moved[row + a - REACH]
        for row in range(ROWS):
            out_ref[channels, block(row)] = sums[row]
        return carry

    lax.fori_loop(0, C // GROUP, conv_group, 0)


def conv_edges(flipped, own_ref, a_ref, b_ref, odd_ref, taps_ref, put):
    odd = odd_ref[0] == 1
    lane = lane_of(GROUP)

    def conv_group(index, carry):
        group = pl.multiple_of(index * GROUP, GROUP)
        channels = pl.ds(group, GROUP)
        rows = outer_rows(group, a_ref, b_ref, odd, NEAR if flipped else WIDE)
        sums = [own_ref[channels, block(row)] for row in range(ROWS)]
        for b in range(KS):
            moved = {at: shifted_row(*row, lane, b - REACH) for at, row in rows.items()}
            for a in range(KS):
                if a == REACH:
                    continue
                weight = tap_of(taps_ref, tap_index(a, b, flipped), group)
                for row in range(ROWS):
                    if row + a - REACH in moved:
                        sums[row] = sums[row] + weight * moved[row + a - REACH]
        put(group, sums)
        return carry

    lax.fori_loop(0, C // GROUP, conv_group, 0)


SPAN = 3 * REACH


def side_sums(side, pieces, taps_ref, group, lane):
    packed = jnp.zeros((GROUP, LANES), F32)
    for place, at in enumerate(sorted(pieces)):
        row, strip, index = pieces[at]
        start = SPAN * place
        if side == 0:
            parts = ((strip, ACTS_REACH * index, start, ACTS_REACH), (row, 0, start + ACTS_REACH, REACH))
        else:
            parts = ((row, LANES - REACH, start, REACH), (strip, ACTS_SIDE + ACTS_REACH * index, start + REACH, ACTS_REACH))
        for value, origin, to, width in parts:
            packed = jnp.where((lane >= to) & (lane < to + width), roll(value, to - origin), packed)
    total = jnp.zeros((GROUP, LANES), F32)
    for tap in range(TAPS):
        total = total + tap_of(taps_ref, tap, group) * roll(packed, -(SPAN * (tap // KS) + tap % KS))
    result = jnp.zeros((GROUP, LANES), F32)
    for row in range(ROWS):
        to = SIDE * side + REACH * row
        result = jnp.where((lane >= to) & (lane < to + REACH), roll(total, to - SPAN * row), result)
    return result


def forward(
    field_ref, strip_ref, own_ref, a_ref, b_ref, odd_ref, taps_ref, gain_ref, bias_ref, w_in_ref, b_in_ref,
    normed_ref, inv_ref, slope_ref, hidden_ref, side_normed_ref, side_inv_ref, side_slope_ref,
):
    def put(group, sums):
        for row in range(ROWS):
            normed_ref[pl.ds(group, GROUP), block(row)] = sums[row]

    conv_edges(False, own_ref, a_ref, b_ref, odd_ref, taps_ref, put)
    odd = odd_ref[0] == 1
    lane = lane_of(GROUP)

    def side_group(index, carry):
        group = pl.multiple_of(index * GROUP, GROUP)
        channels = pl.ds(group, GROUP)
        pieces = outer_pieces(group, a_ref, b_ref, odd) | own_pieces(channels, field_ref, strip_ref)
        left, right = (side_sums(side, pieces, taps_ref, group, lane) for side in range(2))
        side_normed_ref[channels, :] = left + right
        return carry

    lax.fori_loop(0, C // GROUP, side_group, 0)
    w_in = split(w_in_ref[...])

    def finish_cells(conv_out):
        centred = conv_out - jnp.mean(conv_out, axis=0, keepdims=True)
        inv = lax.rsqrt(jnp.mean(centred * centred, axis=0, keepdims=True) + EPSILON)
        normed = centred * inv
        lifted = normed * gain_ref[...] + bias_ref[...]
        pre_act = product(w_in, split(lifted), COL_COL) + b_in_ref[...]
        gate = 0.5 * (1.0 + lax.erf(pre_act * 0.7071067811865476))
        slope = gate + pre_act * jnp.exp(-0.5 * pre_act * pre_act) * 0.3989422804014327
        return normed, inv, slope, pre_act * gate

    for start in range(0, CELLS, CHUNK):
        cells = pl.ds(start, CHUNK)
        normed_ref[:, cells], inv_ref[:, cells], slope_ref[:, cells], hidden_ref[:, cells] = finish_cells(normed_ref[:, cells])
    side_normed_ref[...], side_inv_ref[...], side_slope_ref[...], unused = finish_cells(side_normed_ref[...])


def grad_at(cotan, w_out, w_in, normed, inv, slope):
    grad_pre = product(w_out, split(cotan), ROW_COL) * slope
    grad_normed = product(w_in, split(grad_pre), ROW_COL)
    mean = jnp.mean(grad_normed, axis=0, keepdims=True)
    along = jnp.mean(grad_normed * normed, axis=0, keepdims=True)
    return grad_pre, inv * (grad_normed - mean - normed * along)


def step_tile(cotan_refs, saved, grad_ref, keep):
    normed_ref, inv_ref, slope_ref, w_in_gain_ref, w_out_scale_ref = saved
    w_out = split(w_out_scale_ref[...])
    w_in = split(w_in_gain_ref[...])
    for start in range(0, CELLS, CHUNK):
        cells = pl.ds(start, CHUNK)
        cotan = sum(ref[:, cells] for ref in cotan_refs)
        grad_pre, grad = grad_at(cotan, w_out, w_in, normed_ref[:, cells], inv_ref[:, cells], slope_ref[:, cells])
        keep(cells, cotan, grad_pre)
        grad_ref[:, cells] = grad
    return w_out, w_in


def ignore(cells, cotan, grad_pre):
    pass


def step_sides(lefts, rights, weights, strips):
    left, right = sum(ref[...] for ref in lefts), sum(ref[...] for ref in rights)
    normed_ref, inv_ref, slope_ref = strips
    cotan = unfold(left, right)
    return grad_at(cotan, *weights, normed_ref[...], inv_ref[...], slope_ref[...])[1]


def middle_step(cotan_ref, from_left, from_right, odd_ref, *refs):
    saved, strips, (grad_ref, strip_ref, a_ref, b_ref) = refs[:5], refs[5:8], refs[8:]
    weights = step_tile((cotan_ref,), saved, grad_ref, ignore)
    strip_ref[...] = step_sides((from_left,), (from_right,), weights, strips)
    write_messages(grad_ref, strip_ref, odd_ref, a_ref, b_ref)


def last_step(count, *refs):
    cotans, lefts, rights, odd_ref = refs[:count], refs[count : 2 * count], refs[2 * count : 3 * count], refs[3 * count]
    refs = refs[3 * count + 1 :]
    saved, strips = refs[:5], refs[5:8]
    grad_ref, strip_ref, a_ref, b_ref, cotan_ref, grad_pre_ref = refs[8:]

    def keep(cells, cotan, grad_pre):
        cotan_ref[:, cells] = cotan
        grad_pre_ref[:, cells] = grad_pre

    weights = step_tile(cotans, saved, grad_ref, keep)
    strip_ref[...] = step_sides(lefts, rights, weights, strips)
    write_messages(grad_ref, strip_ref, odd_ref, a_ref, b_ref)


def finish(own_ref, a_ref, b_ref, odd_ref, taps_ref, out_ref, right_ref, left_ref):
    def put(group, sums):
        for row in range(ROWS):
            out_ref[pl.ds(group, GROUP), block(row)] = sums[row]

    conv_edges(True, own_ref, a_ref, b_ref, odd_ref, taps_ref, put)
    pack_edges(out_ref, right_ref, left_ref)


def last_finish(own_ref, a_ref, b_ref, odd_ref, taps_ref, out_ref):
    def put(group, sums):
        for row in range(ROWS):
            out_ref[pl.ds(group * ROWS + row, GROUP, stride=ROWS), :] = sums[row]

    conv_edges(True, own_ref, a_ref, b_ref, odd_ref, taps_ref, put)


LIFT_ROWS = C + GROUP
OUT_AT = 0
IN_AT = OUT_AT + C * HID // LANES
TAPS_AT = IN_AT + LIFT_ROWS * HID // LANES
USED_ROWS = TAPS_AT + C


def parameter_terms(
    field_ref, strip_ref, a_ref, b_ref, odd_ref, grad_ref, cotan_ref, hidden_ref, normed_ref, grad_pre_ref,
    gain_ref, bias_ref, scale_ref, w_in_ref, w_out_ref,
    payload_ref,
):
    odd = odd_ref[0] == 1
    lane = lane_of(GROUP)

    def taps_group(index, carry):
        group = pl.multiple_of(index * GROUP, GROUP)
        found = outer_rows(group, a_ref, b_ref, odd, WIDE) | own_rows(pl.ds(group, GROUP), field_ref, strip_ref, WIDE)
        rows = [found[row] for row in sorted(found)]
        grads = [grad_ref[pl.ds(group, GROUP), block(row)] for row in range(ROWS)]
        result = jnp.zeros((GROUP, LANES), F32)
        for b in range(KS):
            moved = [shifted_row(*row, lane, b - REACH) for row in rows]
            for a in range(KS):
                terms = [grads[row] * moved[row + a] for row in range(ROWS)]
                while len(terms) > 1:
                    terms = [one + two for one, two in zip(terms[0::2], terms[1::2])]
                total = jnp.sum(terms[0], axis=1, keepdims=True)
                result = jnp.where(lane == a * KS + b, total, result)
        payload_ref[pl.ds(TAPS_AT + group, GROUP), :] = result
        return carry

    lax.fori_loop(0, C // GROUP, taps_group, 0)
    grad_w_out = product(split(cotan_ref[...]), split(hidden_ref[...]), ROW_ROW)
    ones = jnp.where(lax.broadcasted_iota(jnp.int32, (GROUP, CELLS), 0) == 0, 1.0, 0.0)
    lifted = jnp.concatenate([normed_ref[...], ones], axis=0)
    grad_w_in = product(split(lifted), split(grad_pre_ref[...]), ROW_ROW)
    grad_b_in = grad_w_in[C : C + 1, :]
    columns = (w_in_ref[...] * grad_w_in[:C, :], w_in_ref[...] * grad_b_in, w_out_ref[...] * grad_w_out)
    lane = lane_of(C)
    for index, terms in enumerate(columns):
        total = jnp.sum(terms, axis=1, keepdims=True)
        taps = payload_ref[pl.ds(TAPS_AT, C), :]
        payload_ref[pl.ds(TAPS_AT, C), :] = jnp.where(lane == TAPS + index, total, taps)
    grad_w_out = grad_w_out * scale_ref[...]
    grad_weights = grad_w_in[:C, :] * gain_ref[...] + bias_ref[...] * grad_b_in
    for part in range(HID // LANES):
        lanes = slice(part * LANES, (part + 1) * LANES)
        at = IN_AT + part * LIFT_ROWS
        payload_ref[pl.ds(OUT_AT + part * C, C), :] = grad_w_out[:, lanes]
        payload_ref[pl.ds(at, C), :] = grad_weights[:, lanes]
        payload_ref[pl.ds(at + C, GROUP), :] = grad_w_in[C:, lanes]
    payload_ref[pl.ds(USED_ROWS, PAYLOAD_ROWS - USED_ROWS), :] = jnp.zeros((PAYLOAD_ROWS - USED_ROWS, LANES), F32)


def sum_shares(shares_ref, out_ref):
    devices = out_ref.shape[0]
    terms = [shares_ref[device] for device in range(devices)]
    while len(terms) > 1:
        terms = [one + two for one, two in zip(terms[0::2], terms[1::2])]
    for device in range(devices):
        out_ref[device] = terms[0]


def parameter_grads(
    payload_ref,
    kernel_out, gain_out, bias_out, w_in_out, b_in_out, w_out_out, scale_out,
):
    by_tap = payload_ref[pl.ds(TAPS_AT, C), :].T
    kernel_out[:, 0, :] = by_tap[:TAPS, :]
    for index, out_ref in enumerate((gain_out, bias_out, scale_out)):
        out_ref[...] = by_tap[TAPS + index : TAPS + index + 1, :]
    for part in range(HID // LANES):
        hidden = pl.ds(part * LANES, LANES)
        at = IN_AT + part * LIFT_ROWS
        w_out_out[:, hidden] = payload_ref[pl.ds(OUT_AT + part * C, C), :]
        w_in_out[:, hidden] = payload_ref[pl.ds(at, C), :]
        b_in_out[:, hidden] = payload_ref[pl.ds(at + C, 1), :]


def pairs(axis, sections, odd_pairs):
    size = lax.axis_size(axis)
    routes = []
    for section in sections:
        for tile in range(1 if odd_pairs else 0, size - 1, 2):
            here = section * size + tile
            routes += [(here, here + 1), (here + 1, here)]
    return routes


def swap_rows(message_a, message_b, sections):
    axes = ("section", "ty")
    return (
        lax.ppermute(message_a, axes, pairs("ty", sections, False)),
        lax.ppermute(message_b, axes, pairs("ty", sections, True)),
    )


def to_sides(to_right, to_left, sections, back=0):
    size = lax.axis_size("tx")
    right = [(s * size + i, (s - back) * size + i + 1) for s in sections for i in range(size - 1)]
    left = [(s * size + i + 1, (s - back) * size + i) for s in sections for i in range(size - 1)]
    axes = ("section", "tx")
    return lax.ppermute(to_right, axes, right), lax.ppermute(to_left, axes, left)


def sum_over_tiles(payload):
    devices = lax.axis_size(TILES)
    shares = lax.all_to_all(payload.reshape(devices, PAYLOAD_ROWS // devices, LANES), TILES, 0, 0)
    (copies,) = call(sum_shares, [shares.shape], shares)
    return lax.all_to_all(copies, TILES, 0, 0).reshape(PAYLOAD_ROWS, LANES)


def on_device(acts, top_grad, kernel, ln_gain, ln_bias, w_in, b_in, w_out, layer_scale):
    sections = lax.axis_size("section")
    every = range(sections)
    is_last = (lax.axis_index("section") == sections - 1).astype(F32)
    odd = lax.rem(lax.axis_index("ty"), 2).astype(jnp.int32).reshape(1)
    field_shape, side, wide, hidden_shape = ((C, CELLS), (FOLD, LANES), (C, LANES), (HID, CELLS))
    edge_outs = [wide, MESSAGE, MESSAGE]
    acts_rows, top_rows = (acts.reshape(C * ROWS, LANES), top_grad.reshape(C * ROWS, LANES))

    field, cotan, to_right, to_left = call(
        take_fields, [field_shape, field_shape, SIDE_MESSAGE, SIDE_MESSAGE], acts_rows, top_rows
    )
    left, right = to_sides(to_right, to_left, every)
    parameters = (
        jnp.transpose(kernel, (1, 0, 2)), ln_gain, ln_bias, w_in[0], b_in, w_out[0].T, layer_scale,
    )
    taps, gain, shift_bias, scale, bias_in, weight_in, weight_out, w_in_gain, w_out_scale = call(
        prepare,
        [(TAPS * C, LANES), (C, 1), (C, 1), (C, 1), (HID, 1), (C, HID), (C, HID), (C, HID), (HID, C)],
        *parameters, scratch=[p.shape for p in parameters] + [pltpu.SemaphoreType.DMA((len(parameters),))], copied=True,
    )
    strip, message_a, message_b = call(edges, edge_outs, field, left, right, odd)
    from_a, from_b = swap_rows(message_a, message_b, every)
    (own,) = call(functools.partial(conv_own, False), [field_shape], field, strip, taps, flops=CONV_FLOPS)
    around = (field, strip, from_a, from_b, odd)
    normed, inv, slope, hidden, *strips = call(
        forward,
        [field_shape, (1, CELLS), hidden_shape, hidden_shape, wide, (1, LANES), (HID, LANES)],
        field, strip, own, from_a, from_b, odd, taps, gain, shift_bias, weight_in, bias_in,
    )
    saved = (normed, inv, slope, w_in_gain, w_out_scale)

    cotan = cotan * is_last
    cotans, lefts, rights = [cotan], [left[ACTS_ROWS:] * is_last], [right[ACTS_ROWS:] * is_last]
    for section in reversed(every):
        only = (section,) if section else every
        if section:
            grad, grad_strip, message_a, message_b = call(
                middle_step, [field_shape] + edge_outs, cotan, lefts[-1], rights[-1], odd, *saved, *strips
            )
        else:
            grad, grad_strip, message_a, message_b, cotan, grad_pre = call(
                functools.partial(last_step, len(cotans)), [field_shape] + edge_outs + [field_shape, hidden_shape],
                *cotans, *lefts, *rights, odd, *saved, *strips,
            )
            (payload,) = call(
                parameter_terms, [(PAYLOAD_ROWS, LANES)],
                *around, grad, cotan, hidden, normed, grad_pre, gain, shift_bias, scale, weight_in, weight_out,
                flops=4 * CONV_FLOPS,
            )
        grad_a, grad_b = swap_rows(message_a, message_b, only)
        (own,) = call(
            functools.partial(conv_own, True), [field_shape], cotan, grad, grad_strip, taps, flops=CONV_FLOPS
        )
        if section:
            cotan, to_right, to_left = call(finish, [field_shape, side, side], own, grad_a, grad_b, odd, taps)
            from_left, from_right = to_sides(to_right, to_left, only, 1)
            cotan = lax.ppermute(cotan, "section", [(section, section - 1)])
            cotans.append(cotan)
            lefts.append(from_left)
            rights.append(from_right)
    payload = sum_over_tiles(payload)
    (input_grad,) = call(last_finish, [(C * ROWS, LANES)], own, grad_a, grad_b, odd, taps)
    grad_kernel, grad_gain, grad_bias, grad_w_in, grad_b_in, grad_w_out, grad_scale = call(
        parameter_grads,
        [(TAPS, 1, C), (1, C), (1, C), (C, HID), (1, HID), (C, HID), (1, C)],
        payload,
    )
    return (
        input_grad.reshape(1, 1, C, ROWS, LANES),
        jnp.transpose(grad_kernel, (1, 0, 2)),
        grad_gain,
        grad_bias,
        grad_w_in[None],
        grad_b_in,
        grad_w_out.T[None],
        grad_scale,
    )


def solution(mesh):
    placed = (
        P("section", None, None, "ty", "tx"),
        P(None, None, "ty", "tx"),
        P("section", None, None),
        P("section", None),
        P("section", None),
        P("section", None, None),
        P("section", None),
        P("section", None, None),
        P("section", None),
    )
    return jax.shard_map(
        on_device,
        mesh=mesh,
        in_specs=placed,
        out_specs=(
            P("section", None, None, "ty", "tx"),
            P("section", None, None),
            P("section", None),
            P("section", None),
            P("section", None, None),
            P("section", None),
            P("section", None, None),
            P("section", None),
        ),
        check_vma=False,
    )
```

```python
import functools

import jax
import jax.numpy as jnp
from jax import lax
from jax.experimental import pallas as pl
from jax.experimental.pallas import tpu as pltpu
from jax.sharding import PartitionSpec as P

KS = 7
TAPS = KS * KS
REACH = KS // 2
EPSILON = 1e-06
LANES = 128
GROUP = 8
ROWS = 8
C = 96
HID = 384
CELLS = ROWS * LANES
FOLD = 24
CHUNK = 256
PAYLOAD_ROWS = 1024
F32 = jnp.float32
BF16 = jnp.bfloat16
CONV_FLOPS = 2 * TAPS * C * CELLS
TILES = ("ty", "tx")


def call(kernel, outs, *operands, scratch=(), flops=0, copied=False):
    whole = pl.BlockSpec(memory_space=pltpu.VMEM)
    specs = [
        pl.BlockSpec(memory_space=pltpu.SMEM if operand.dtype == jnp.int32 else pltpu.HBM if copied else pltpu.VMEM)
        for operand in operands
    ]
    spaces = [pltpu.VMEM(shape, F32) if isinstance(shape, tuple) else shape for shape in scratch]
    return pl.pallas_call(
        kernel,
        out_shape=[jax.ShapeDtypeStruct(shape, F32) for shape in outs],
        in_specs=specs,
        out_specs=[whole] * len(outs),
        scratch_shapes=spaces,
        compiler_params=pltpu.CompilerParams(vmem_limit_bytes=28 * 1024 * 1024),
        cost_estimate=pl.CostEstimate(flops=flops, bytes_accessed=0, transcendentals=0) if flops else None,
    )(*operands)


def roll(value, shift):
    return pltpu.roll(value, shift % LANES, 1)


def lane_of(rows):
    return lax.broadcasted_iota(jnp.int32, (rows, LANES), 1)


def block(row):
    return pl.ds(row * LANES, LANES)


def split(value):
    high = value.astype(BF16)
    low = (value - high.astype(F32)).astype(BF16)
    return high, low


def product(left, right, dims):
    def part(one, two):
        return lax.dot_general(one, two, (dims, ((), ())), preferred_element_type=F32)

    return part(left[0], right[0]) + (part(left[0], right[1]) + part(left[1], right[0]))


ROW_COL = ((1,), (0,))
COL_COL = ((0,), (0,))
ROW_ROW = ((1,), (1,))


ACTS_REACH = 2 * REACH
ACTS_SIDE = 64
SIDE = 32


def pack_edges(field_ref, right_ref, left_ref, width=REACH, side=SIDE):
    rows = out_rows = C * side // LANES
    lane = lane_of(out_rows)
    for edge, out_ref in ((LANES - width, right_ref), (0, left_ref)):
        folded = jnp.zeros((out_rows, LANES), F32)
        for part in range(LANES // side):
            for row in range(ROWS):
                at = side * part + width * row
                moved = roll(field_ref[pl.ds(part * rows, rows), block(row)], at - edge)
                folded = jnp.where((lane >= at) & (lane < at + width), moved, folded)
        out_ref[...] = folded


def unfold(left, right, side=SIDE):
    lane = lane_of(left.shape[0])
    parts = []
    for part in range(LANES // side):
        theirs = roll(left, -side * part)
        parts.append(jnp.where(lane < side, theirs, jnp.where(lane < 2 * side, roll(right, side - side * part), 0.0)))
    return jnp.concatenate(parts, axis=0)


def shifted_row(row, left, right, lane, distance):
    if distance > 0:
        return roll(jnp.where(lane < distance, right, row), -distance)
    if distance < 0:
        return roll(jnp.where(lane >= LANES + distance, left, row), -distance)
    return row


NEAR = (REACH, 0, SIDE)
WIDE = (ACTS_REACH, REACH, ACTS_SIDE)


def with_edges(value, strip, row, layout):
    width, skipped, side = layout
    return value, roll(strip, LANES - REACH - skipped - width * row), roll(strip, -side - width * row)


def tap_of(taps_ref, tap, group):
    return taps_ref[pl.ds(tap * C + group, GROUP), :]


ACTS_ROWS = C * ACTS_SIDE // LANES
SIDE_MESSAGE = (ACTS_ROWS + FOLD, LANES)


def take_fields(acts_ref, top_ref, field_ref, cotan_ref, right_ref, left_ref):
    for row in range(ROWS):
        field_ref[:, block(row)] = acts_ref[pl.ds(row, C, stride=ROWS), :]
        cotan_ref[:, block(row)] = top_ref[pl.ds(row, C, stride=ROWS), :]
    wide, near = pl.ds(0, ACTS_ROWS), pl.ds(ACTS_ROWS, FOLD)
    pack_edges(field_ref, right_ref.at[wide, :], left_ref.at[wide, :], ACTS_REACH, ACTS_SIDE)
    pack_edges(cotan_ref, right_ref.at[near, :], left_ref.at[near, :])


def column(row):
    return jnp.broadcast_to(row, (GROUP, row.shape[1])).T[:, :1]


def prepare(*refs):
    count = 7
    sources, outs, held = refs[: count], refs[count : -count - 1], refs[-count - 1 : -1]
    sems = refs[-1]
    copies = [pltpu.make_async_copy(source, target, sems.at[i]) for i, (source, target) in enumerate(zip(sources, held))]
    for copy in copies:
        copy.start()
    for copy in copies:
        copy.wait()
    kernel_ref, gain_row, bias_row, w_in_ref, b_in_row, w_out_ref, scale_row = held
    taps_ref, gain_ref, bias_ref, scale_ref, b_in_ref, w_in_out, w_out_out, w_in_gain_ref, w_out_scale_ref = outs
    taps = kernel_ref[:, 0, :].T
    for tap in range(TAPS):
        taps_ref[pl.ds(tap * C, C), :] = jnp.broadcast_to(taps[:, tap : tap + 1], (C, LANES))
    gain_ref[...] = column(gain_row[...])
    bias_ref[...] = column(bias_row[...])
    scale_ref[...] = column(scale_row[...])
    b_in_ref[...] = column(b_in_row[...])
    w_in_out[...] = w_in_ref[...]
    w_out_out[...] = w_out_ref[...]
    w_in_gain_ref[...] = w_in_ref[...] * gain_ref[...]
    w_out_scale_ref[...] = (w_out_ref[...] * scale_ref[...]).T


STRIP_AT = REACH * C
MESSAGE = (STRIP_AT + C, LANES)


def write_messages(field_ref, strip_ref, odd_ref, a_ref, b_ref):
    odd = odd_ref[0]
    for first, out_ref in (((1 - odd) * (ROWS - REACH), a_ref), (odd * (ROWS - REACH), b_ref)):
        for index in range(REACH):
            lanes = pl.ds(pl.multiple_of((first + index) * LANES, LANES), LANES)
            out_ref[pl.ds(index * C, C), :] = field_ref[:, lanes]
        out_ref[pl.ds(STRIP_AT, C), :] = strip_ref[...]


def outer_pieces(group, a_ref, b_ref, odd):
    rows = {}
    for index in range(REACH + 1):
        at = pl.ds(index * C + group, GROUP)
        from_a, from_b = a_ref[at, :], b_ref[at, :]
        rows[index] = (jnp.where(odd, from_a, from_b), jnp.where(odd, from_b, from_a))
    above, below = rows.pop(REACH)
    found = {}
    for index in range(REACH):
        found[index - REACH] = (rows[index][0], above, ROWS - REACH + index)
        found[ROWS + index] = (rows[index][1], below, index)
    return found


def outer_rows(group, a_ref, b_ref, odd, layout):
    return {at: with_edges(*piece, layout) for at, piece in outer_pieces(group, a_ref, b_ref, odd).items()}


def own_pieces(channels, field_ref, strip_ref):
    strip = strip_ref[channels, :]
    return {row: (field_ref[channels, block(row)], strip, row) for row in range(ROWS)}


def own_rows(channels, field_ref, strip_ref, layout):
    return {at: with_edges(*piece, layout) for at, piece in own_pieces(channels, field_ref, strip_ref).items()}


def edges(field_ref, left_ref, right_ref, odd_ref, strip_ref, a_ref, b_ref):
    wide = pl.ds(0, ACTS_ROWS)
    strip_ref[...] = unfold(left_ref[wide, :], right_ref[wide, :], ACTS_SIDE)
    write_messages(field_ref, strip_ref, odd_ref, a_ref, b_ref)


def tap_index(a, b, flipped):
    tap = a * KS + b
    return TAPS - 1 - tap if flipped else tap


def conv_own(flipped, *refs):
    start_ref = refs[0] if flipped else None
    field_ref, strip_ref, taps_ref, out_ref = refs[-4:]
    lane = lane_of(GROUP)

    def conv_group(index, carry):
        group = pl.multiple_of(index * GROUP, GROUP)
        channels = pl.ds(group, GROUP)
        rows = own_rows(channels, field_ref, strip_ref, NEAR if flipped else WIDE)
        if flipped:
            sums = [start_ref[channels, block(row)] for row in range(ROWS)]
        else:
            sums = [jnp.zeros((GROUP, LANES), F32)] * ROWS
        for b in range(KS):
            moved = [shifted_row(*rows[row], lane, b - REACH) for row in range(ROWS)]
            for a in range(KS):
                weight = tap_of(taps_ref, tap_index(a, b, flipped), group)
                for row in range(ROWS):
                    if 0 <= row + a - REACH < ROWS:
                        sums[row] = sums[row] + weight * moved[row + a - REACH]
        for row in range(ROWS):
            out_ref[channels, block(row)] = sums[row]
        return carry

    lax.fori_loop(0, C // GROUP, conv_group, 0)


def conv_edges(flipped, own_ref, a_ref, b_ref, odd_ref, taps_ref, put):
    odd = odd_ref[0] == 1
    lane = lane_of(GROUP)

    def conv_group(index, carry):
        group = pl.multiple_of(index * GROUP, GROUP)
        channels = pl.ds(group, GROUP)
        rows = outer_rows(group, a_ref, b_ref, odd, NEAR if flipped else WIDE)
        sums = [own_ref[channels, block(row)] for row in range(ROWS)]
        for b in range(KS):
            moved = {at: shifted_row(*row, lane, b - REACH) for at, row in rows.items()}
            for a in range(KS):
                if a == REACH:
                    continue
                weight = tap_of(taps_ref, tap_index(a, b, flipped), group)
                for row in range(ROWS):
                    if row + a - REACH in moved:
                        sums[row] = sums[row] + weight * moved[row + a - REACH]
        put(group, sums)
        return carry

    lax.fori_loop(0, C // GROUP, conv_group, 0)


SPAN = 3 * REACH


def side_sums(side, pieces, taps_ref, group, lane):
    packed = jnp.zeros((GROUP, LANES), F32)
    for place, at in enumerate(sorted(pieces)):
        row, strip, index = pieces[at]
        start = SPAN * place
        if side == 0:
            parts = ((strip, ACTS_REACH * index, start, ACTS_REACH), (row, 0, start + ACTS_REACH, REACH))
        else:
            parts = ((row, LANES - REACH, start, REACH), (strip, ACTS_SIDE + ACTS_REACH * index, start + REACH, ACTS_REACH))
        for value, origin, to, width in parts:
            packed = jnp.where((lane >= to) & (lane < to + width), roll(value, to - origin), packed)
    sums = [jnp.zeros((GROUP, LANES), F32)] * KS
    for a in range(KS):
        for b in range(KS):
            sums[b] = sums[b] + tap_of(taps_ref, a * KS + b, group) * roll(packed, -(SPAN * a + b))
    total = (sums[0] + sums[1]) + (sums[2] + sums[3]) + ((sums[4] + sums[5]) + sums[6])
    result = jnp.zeros((GROUP, LANES), F32)
    for row in range(ROWS):
        to = SIDE * side + REACH * row
        result = jnp.where((lane >= to) & (lane < to + REACH), roll(total, to - SPAN * row), result)
    return result


def forward(
    field_ref, strip_ref, own_ref, a_ref, b_ref, odd_ref, taps_ref, gain_ref, bias_ref, w_in_ref, b_in_ref,
    normed_ref, inv_ref, slope_ref, hidden_ref, side_normed_ref, side_inv_ref, side_slope_ref,
):
    def put(group, sums):
        for row in range(ROWS):
            normed_ref[pl.ds(group, GROUP), block(row)] = sums[row]

    conv_edges(False, own_ref, a_ref, b_ref, odd_ref, taps_ref, put)
    odd = odd_ref[0] == 1
    lane = lane_of(GROUP)

    def side_group(index, carry):
        group = pl.multiple_of(index * GROUP, GROUP)
        channels = pl.ds(group, GROUP)
        pieces = outer_pieces(group, a_ref, b_ref, odd) | own_pieces(channels, field_ref, strip_ref)
        left, right = (side_sums(side, pieces, taps_ref, group, lane) for side in range(2))
        side_normed_ref[channels, :] = left + right
        return carry

    lax.fori_loop(0, C // GROUP, side_group, 0)
    w_in = split(w_in_ref[...])

    def finish_cells(conv_out):
        centred = conv_out - jnp.mean(conv_out, axis=0, keepdims=True)
        inv = lax.rsqrt(jnp.mean(centred * centred, axis=0, keepdims=True) + EPSILON)
        normed = centred * inv
        lifted = normed * gain_ref[...] + bias_ref[...]
        pre_act = product(w_in, split(lifted), COL_COL) + b_in_ref[...]
        gate = 0.5 * (1.0 + lax.erf(pre_act * 0.7071067811865476))
        slope = gate + pre_act * jnp.exp(-0.5 * pre_act * pre_act) * 0.3989422804014327
        return normed, inv, slope, pre_act * gate

    for start in range(0, CELLS, CHUNK):
        cells = pl.ds(start, CHUNK)
        normed_ref[:, cells], inv_ref[:, cells], slope_ref[:, cells], hidden_ref[:, cells] = finish_cells(normed_ref[:, cells])
    side_normed_ref[...], side_inv_ref[...], side_slope_ref[...], unused = finish_cells(side_normed_ref[...])


def grad_at(cotan, w_out, w_in, normed, inv, slope):
    grad_pre = product(w_out, split(cotan), ROW_COL) * slope
    grad_normed = product(w_in, split(grad_pre), ROW_COL)
    mean = jnp.mean(grad_normed, axis=0, keepdims=True)
    along = jnp.mean(grad_normed * normed, axis=0, keepdims=True)
    return grad_pre, inv * (grad_normed - mean - normed * along)


def step_tile(cotan_refs, saved, grad_ref, keep):
    normed_ref, inv_ref, slope_ref, w_in_gain_ref, w_out_scale_ref = saved
    w_out = split(w_out_scale_ref[...])
    w_in = split(w_in_gain_ref[...])
    for start in range(0, CELLS, CHUNK):
        cells = pl.ds(start, CHUNK)
        cotan = sum(ref[:, cells] for ref in cotan_refs)
        grad_pre, grad = grad_at(cotan, w_out, w_in, normed_ref[:, cells], inv_ref[:, cells], slope_ref[:, cells])
        keep(cells, cotan, grad_pre)
        grad_ref[:, cells] = grad
    return w_out, w_in


def ignore(cells, cotan, grad_pre):
    pass


def step_sides(lefts, rights, weights, strips):
    left, right = sum(ref[...] for ref in lefts), sum(ref[...] for ref in rights)
    normed_ref, inv_ref, slope_ref = strips
    cotan = unfold(left, right)
    return grad_at(cotan, *weights, normed_ref[...], inv_ref[...], slope_ref[...])[1]


def middle_step(cotan_ref, from_left, from_right, odd_ref, *refs):
    saved, strips, (grad_ref, strip_ref, a_ref, b_ref) = refs[:5], refs[5:8], refs[8:]
    weights = step_tile((cotan_ref,), saved, grad_ref, ignore)
    strip_ref[...] = step_sides((from_left,), (from_right,), weights, strips)
    write_messages(grad_ref, strip_ref, odd_ref, a_ref, b_ref)


def last_step(count, *refs):
    cotans, lefts, rights, odd_ref = refs[:count], refs[count : 2 * count], refs[2 * count : 3 * count], refs[3 * count]
    refs = refs[3 * count + 1 :]
    saved, strips = refs[:5], refs[5:8]
    grad_ref, strip_ref, a_ref, b_ref, cotan_ref, grad_pre_ref = refs[8:]

    def keep(cells, cotan, grad_pre):
        cotan_ref[:, cells] = cotan
        grad_pre_ref[:, cells] = grad_pre

    weights = step_tile(cotans, saved, grad_ref, keep)
    strip_ref[...] = step_sides(lefts, rights, weights, strips)
    write_messages(grad_ref, strip_ref, odd_ref, a_ref, b_ref)


def finish(own_ref, a_ref, b_ref, odd_ref, taps_ref, out_ref, right_ref, left_ref):
    def put(group, sums):
        for row in range(ROWS):
            out_ref[pl.ds(group, GROUP), block(row)] = sums[row]

    conv_edges(True, own_ref, a_ref, b_ref, odd_ref, taps_ref, put)
    pack_edges(out_ref, right_ref, left_ref)


def last_finish(own_ref, a_ref, b_ref, odd_ref, taps_ref, out_ref):
    def put(group, sums):
        for row in range(ROWS):
            out_ref[pl.ds(group * ROWS + row, GROUP, stride=ROWS), :] = sums[row]

    conv_edges(True, own_ref, a_ref, b_ref, odd_ref, taps_ref, put)


LIFT_ROWS = C + GROUP
OUT_AT = 0
IN_AT = OUT_AT + C * HID // LANES
TAPS_AT = IN_AT + LIFT_ROWS * HID // LANES
USED_ROWS = TAPS_AT + C


def parameter_terms(
    field_ref, strip_ref, a_ref, b_ref, odd_ref, grad_ref, cotan_ref, hidden_ref, normed_ref, grad_pre_ref,
    gain_ref, bias_ref, scale_ref, w_in_ref, w_out_ref,
    payload_ref,
):
    odd = odd_ref[0] == 1
    lane = lane_of(GROUP)

    def taps_group(index, carry):
        group = pl.multiple_of(index * GROUP, GROUP)
        found = outer_rows(group, a_ref, b_ref, odd, WIDE) | own_rows(pl.ds(group, GROUP), field_ref, strip_ref, WIDE)
        rows = [found[row] for row in sorted(found)]
        grads = [grad_ref[pl.ds(group, GROUP), block(row)] for row in range(ROWS)]
        result = jnp.zeros((GROUP, LANES), F32)
        for b in range(KS):
            moved = [shifted_row(*row, lane, b - REACH) for row in rows]
            for a in range(KS):
                terms = [grads[row] * moved[row + a] for row in range(ROWS)]
                while len(terms) > 1:
                    terms = [one + two for one, two in zip(terms[0::2], terms[1::2])]
                total = jnp.sum(terms[0], axis=1, keepdims=True)
                result = jnp.where(lane == a * KS + b, total, result)
        payload_ref[pl.ds(TAPS_AT + group, GROUP), :] = result
        return carry

    lax.fori_loop(0, C // GROUP, taps_group, 0)
    grad_w_out = product(split(cotan_ref[...]), split(hidden_ref[...]), ROW_ROW)
    ones = jnp.where(lax.broadcasted_iota(jnp.int32, (GROUP, CELLS), 0) == 0, 1.0, 0.0)
    lifted = jnp.concatenate([normed_ref[...], ones], axis=0)
    grad_w_in = product(split(lifted), split(grad_pre_ref[...]), ROW_ROW)
    grad_b_in = grad_w_in[C : C + 1, :]
    columns = (w_in_ref[...] * grad_w_in[:C, :], w_in_ref[...] * grad_b_in, w_out_ref[...] * grad_w_out)
    lane = lane_of(C)
    for index, terms in enumerate(columns):
        total = jnp.sum(terms, axis=1, keepdims=True)
        taps = payload_ref[pl.ds(TAPS_AT, C), :]
        payload_ref[pl.ds(TAPS_AT, C), :] = jnp.where(lane == TAPS + index, total, taps)
    grad_w_out = grad_w_out * scale_ref[...]
    grad_weights = grad_w_in[:C, :] * gain_ref[...] + bias_ref[...] * grad_b_in
    for part in range(HID // LANES):
        lanes = slice(part * LANES, (part + 1) * LANES)
        at = IN_AT + part * LIFT_ROWS
        payload_ref[pl.ds(OUT_AT + part * C, C), :] = grad_w_out[:, lanes]
        payload_ref[pl.ds(at, C), :] = grad_weights[:, lanes]
        payload_ref[pl.ds(at + C, GROUP), :] = grad_w_in[C:, lanes]
    payload_ref[pl.ds(USED_ROWS, PAYLOAD_ROWS - USED_ROWS), :] = jnp.zeros((PAYLOAD_ROWS - USED_ROWS, LANES), F32)


def sum_shares(shares_ref, out_ref):
    devices = out_ref.shape[0]
    terms = [shares_ref[device] for device in range(devices)]
    while len(terms) > 1:
        terms = [one + two for one, two in zip(terms[0::2], terms[1::2])]
    for device in range(devices):
        out_ref[device] = terms[0]


def parameter_grads(
    payload_ref,
    kernel_out, gain_out, bias_out, w_in_out, b_in_out, w_out_out, scale_out,
):
    by_tap = payload_ref[pl.ds(TAPS_AT, C), :].T
    kernel_out[:, 0, :] = by_tap[:TAPS, :]
    for index, out_ref in enumerate((gain_out, bias_out, scale_out)):
        out_ref[...] = by_tap[TAPS + index : TAPS + index + 1, :]
    for part in range(HID // LANES):
        hidden = pl.ds(part * LANES, LANES)
        at = IN_AT + part * LIFT_ROWS
        w_out_out[:, hidden] = payload_ref[pl.ds(OUT_AT + part * C, C), :]
        w_in_out[:, hidden] = payload_ref[pl.ds(at, C), :]
        b_in_out[:, hidden] = payload_ref[pl.ds(at + C, 1), :]


def pairs(axis, sections, odd_pairs):
    size = lax.axis_size(axis)
    routes = []
    for section in sections:
        for tile in range(1 if odd_pairs else 0, size - 1, 2):
            here = section * size + tile
            routes += [(here, here + 1), (here + 1, here)]
    return routes


def swap_rows(message_a, message_b, sections):
    axes = ("section", "ty")
    return (
        lax.ppermute(message_a, axes, pairs("ty", sections, False)),
        lax.ppermute(message_b, axes, pairs("ty", sections, True)),
    )


def to_sides(to_right, to_left, sections, back=0):
    size = lax.axis_size("tx")
    right = [(s * size + i, (s - back) * size + i + 1) for s in sections for i in range(size - 1)]
    left = [(s * size + i + 1, (s - back) * size + i) for s in sections for i in range(size - 1)]
    axes = ("section", "tx")
    return lax.ppermute(to_right, axes, right), lax.ppermute(to_left, axes, left)


def sum_over_tiles(payload):
    devices = lax.axis_size(TILES)
    shares = lax.all_to_all(payload.reshape(devices, PAYLOAD_ROWS // devices, LANES), TILES, 0, 0)
    (copies,) = call(sum_shares, [shares.shape], shares)
    return lax.all_to_all(copies, TILES, 0, 0).reshape(PAYLOAD_ROWS, LANES)


def on_device(acts, top_grad, kernel, ln_gain, ln_bias, w_in, b_in, w_out, layer_scale):
    sections = lax.axis_size("section")
    every = range(sections)
    is_last = (lax.axis_index("section") == sections - 1).astype(F32)
    odd = lax.rem(lax.axis_index("ty"), 2).astype(jnp.int32).reshape(1)
    field_shape, side, wide, hidden_shape = ((C, CELLS), (FOLD, LANES), (C, LANES), (HID, CELLS))
    edge_outs = [wide, MESSAGE, MESSAGE]
    acts_rows, top_rows = (acts.reshape(C * ROWS, LANES), top_grad.reshape(C * ROWS, LANES))

    field, cotan, to_right, to_left = call(
        take_fields, [field_shape, field_shape, SIDE_MESSAGE, SIDE_MESSAGE], acts_rows, top_rows
    )
    left, right = to_sides(to_right, to_left, every)
    parameters = (
        jnp.transpose(kernel, (1, 0, 2)), ln_gain, ln_bias, w_in[0], b_in, w_out[0].T, layer_scale,
    )
    taps, gain, shift_bias, scale, bias_in, weight_in, weight_out, w_in_gain, w_out_scale = call(
        prepare,
        [(TAPS * C, LANES), (C, 1), (C, 1), (C, 1), (HID, 1), (C, HID), (C, HID), (C, HID), (HID, C)],
        *parameters, scratch=[p.shape for p in parameters] + [pltpu.SemaphoreType.DMA((len(parameters),))], copied=True,
    )
    strip, message_a, message_b = call(edges, edge_outs, field, left, right, odd)
    from_a, from_b = swap_rows(message_a, message_b, every)
    (own,) = call(functools.partial(conv_own, False), [field_shape], field, strip, taps, flops=CONV_FLOPS)
    around = (field, strip, from_a, from_b, odd)
    normed, inv, slope, hidden, *strips = call(
        forward,
        [field_shape, (1, CELLS), hidden_shape, hidden_shape, wide, (1, LANES), (HID, LANES)],
        field, strip, own, from_a, from_b, odd, taps, gain, shift_bias, weight_in, bias_in,
    )
    saved = (normed, inv, slope, w_in_gain, w_out_scale)

    cotan = cotan * is_last
    cotans, lefts, rights = [cotan], [left[ACTS_ROWS:] * is_last], [right[ACTS_ROWS:] * is_last]
    for section in reversed(every):
        only = (section,) if section else every
        if section:
            grad, grad_strip, message_a, message_b = call(
                middle_step, [field_shape] + edge_outs, cotan, lefts[-1], rights[-1], odd, *saved, *strips
            )
        else:
            grad, grad_strip, message_a, message_b, cotan, grad_pre = call(
                functools.partial(last_step, len(cotans)), [field_shape] + edge_outs + [field_shape, hidden_shape],
                *cotans, *lefts, *rights, odd, *saved, *strips,
            )
            (payload,) = call(
                parameter_terms, [(PAYLOAD_ROWS, LANES)],
                *around, grad, cotan, hidden, normed, grad_pre, gain, shift_bias, scale, weight_in, weight_out,
                flops=4 * CONV_FLOPS,
            )
        grad_a, grad_b = swap_rows(message_a, message_b, only)
        (own,) = call(
            functools.partial(conv_own, True), [field_shape], cotan, grad, grad_strip, taps, flops=CONV_FLOPS
        )
        if section:
            cotan, to_right, to_left = call(finish, [field_shape, side, side], own, grad_a, grad_b, odd, taps)
            from_left, from_right = to_sides(to_right, to_left, only, 1)
            cotan = lax.ppermute(cotan, "section", [(section, section - 1)])
            cotans.append(cotan)
            lefts.append(from_left)
            rights.append(from_right)
    payload = sum_over_tiles(payload)
    (input_grad,) = call(last_finish, [(C * ROWS, LANES)], own, grad_a, grad_b, odd, taps)
    grad_kernel, grad_gain, grad_bias, grad_w_in, grad_b_in, grad_w_out, grad_scale = call(
        parameter_grads,
        [(TAPS, 1, C), (1, C), (1, C), (C, HID), (1, HID), (C, HID), (1, C)],
        payload,
    )
    return (
        input_grad.reshape(1, 1, C, ROWS, LANES),
        jnp.transpose(grad_kernel, (1, 0, 2)),
        grad_gain,
        grad_bias,
        grad_w_in[None],
        grad_b_in,
        grad_w_out.T[None],
        grad_scale,
    )


def solution(mesh):
    placed = (
        P("section", None, None, "ty", "tx"),
        P(None, None, "ty", "tx"),
        P("section", None, None),
        P("section", None),
        P("section", None),
        P("section", None, None),
        P("section", None),
        P("section", None, None),
        P("section", None),
    )
    return jax.shard_map(
        on_device,
        mesh=mesh,
        in_specs=placed,
        out_specs=(
            P("section", None, None, "ty", "tx"),
            P("section", None, None),
            P("section", None),
            P("section", None),
            P("section", None, None),
            P("section", None),
            P("section", None, None),
            P("section", None),
        ),
        check_vma=False,
    )
```
